256 devices in a mesh: rep: 32 (over x_lo, z, core), fsdp: 8 (over y, x_hi).
Axes of the slice: x: 4 (x_hi: 2, x_lo: 2; x = x_hi * 2 + x_lo), y: 4, z: 8, core: 2. Of those that a mesh axis runs over, the one named last changes fastest.
Arguments:
- activations: bfloat16 [32, 3072, 8192], P('rep', 'fsdp'), may hold values from -6 to 6
- norm_gain: float32 [8192], replicated, may hold values from 0.1 to 1.9
- key_weight: bfloat16 [32, 8192, 512], P('rep', 'fsdp'), may hold values from -0.03125 to 0.03125
- key_target: bfloat16 [32, 3072, 512], P('rep', 'fsdp'), may hold values from -1.5 to 1.5
- replica_frag: bfloat16 [32, 8192, 1024], P('rep', 'fsdp'), may hold values from -1.5 to 1.5
- outer_params: float32 [8192, 1024], P(('fsdp', 'rep')), may hold values from -1.5 to 1.5
- outer_moment: float32 [8192, 1024], P(('fsdp', 'rep')), may hold values from -0.6 to 0.6
Outputs:
- new_params: float32 [8192, 1024], P(('fsdp', 'rep'))
- new_moment: float32 [8192, 1024], P(('fsdp', 'rep'))
- fresh_frag: bfloat16 [8192, 1024], P('fsdp')
- weight_grad: bfloat16 [32, 8192, 512], P('rep', 'fsdp')
The draws below stay inside these ranges and needn't reach their ends.
All inputs are finite; a program needn't handle non-finite values.
Results may differ from the reference program's by a relative error of at most 0.015.
Values may be sent and summed in bfloat16 or wider, within the bound.
No kernel may reach another device: no remote copies, remote signals or barrier semaphores. Data moves between devices by JAX's collectives and lax.ppermute only.
A program may use at most 128 MiB of HBM per device.

```python
import jax
import jax.numpy as jnp
from jax import lax

D = 8192
BLOCK = 128
TOK_DEV = 384
KF = 1024
KI = 512
REPS = 32
TOKENS = 3072
N_FSDP = 8


def spiked(entries, stream_key, source, target, shards_of, factor):
    def block_of(axis_at):
        return (jnp.arange(entries.shape[axis_at]) // (entries.shape[axis_at] // shards_of)).reshape((-1,) + (1,) * (entries.ndim - 1 - axis_at))

    one_side = jax.random.permutation(stream_key, shards_of)[block_of(target)]
    other_side = (block_of(target) + shards_of // 2) % shards_of
    return jnp.where((block_of(source) == one_side) | (block_of(source) == other_side), factor * entries, entries)


def shard_levels(own_key, dims, pieces, low, top_value):
    level = 1.0
    for axis_at, shards_of in pieces:
        heights = jax.random.uniform(jax.random.fold_in(jax.random.fold_in(own_key, 6), axis_at), (shards_of,), jnp.float32, low / len(pieces), top_value / len(pieces))
        level = level * jnp.repeat(jnp.exp(heights), dims[axis_at] // shards_of).reshape((-1,) + (1,) * (len(dims) - 1 - axis_at))
    return level


def normal_values(rng, dims, scale, limit, split=(), kind=jnp.bfloat16):
    values = scale * jax.random.normal(rng, dims, jnp.float32)
    if split:
        values = values * shard_levels(rng, dims, split, -0.22, 0.18)
    return jnp.clip(values, -limit, limit).astype(kind)


def bell_draw_with(key, dims, scale, bound, split, heavy, held_as=jnp.bfloat16):
    drawn = scale * jax.random.normal(key, dims, jnp.float32)
    if split:
        drawn = drawn * shard_levels(key, dims, split, -0.22, 0.18)
    return jnp.clip(spiked(drawn, jax.random.fold_in(key, 3), *heavy), -bound, bound).astype(held_as)


def setup_inputs(seed: int = 0) -> dict:
    splits = jax.random.split(jax.random.key(seed), 8)
    activations = normal_values(splits[0], (REPS, TOKENS, D), 1.0, 6.0, ((0, 32), (1, 8)))
    norm_gain = jnp.clip(1.0 + 0.18 * jax.random.normal(splits[1], (D,), jnp.float32), 0.1, 1.9)
    key_weight = normal_values(splits[2], (REPS, D, KI), (4 * D) ** -0.5, 0.03125, ((0, 32), (1, 8)))
    key_target = normal_values(splits[3], (REPS, TOKENS, KI), 0.25, 1.5, ((0, 32), (1, 8)))
    replica_frag = bell_draw_with(splits[4], (REPS, D, KF), 0.25, 1.5, ((0, 32), (1, 8)), (0, 1, 32, 2.75))
    outer_params = normal_values(splits[5], (D, KF), 0.25, 1.5, ((0, 256),), jnp.float32)
    outer_moment = normal_values(splits[6], (D, KF), 0.1, 0.6, ((0, 256),), jnp.float32)
    return {"activations": activations, "norm_gain": norm_gain, "key_weight": key_weight, "key_target": key_target, "replica_frag": replica_frag, "outer_params": outer_params, "outer_moment": outer_moment}


def encode_blocks(deltas):
    shaped = deltas.reshape(deltas.shape[:-1] + (deltas.shape[-1] // BLOCK, BLOCK))
    needed = (lax.optimization_barrier(jnp.max(jnp.abs(shaped), axis=-1, keepdims=True)) + 1e-06) / 448.0
    scales = jnp.full(needed.shape, 2.0 ** 9, needed.dtype)
    for exponent in range(8, -31, -1):
        scales = jnp.where(needed <= 2.0 ** exponent, 2.0 ** exponent, scales)
    magnitude = jnp.abs(shaped) / scales
    spacing = jnp.full(magnitude.shape, 2.0 ** (-9), magnitude.dtype)
    for exponent in range(-5, 9):
        spacing = jnp.where(magnitude >= 2.0 ** exponent, 2.0 ** (exponent - 3), spacing)
    levels = jnp.floor(magnitude / spacing + 0.5) * spacing
    encoded = jnp.where(shaped < 0, -levels, levels).astype(jnp.bfloat16)
    return (encoded, scales)

def decode_rows(deltas):
    encoded, scales = encode_blocks(deltas)
    return (encoded.astype(jnp.float32) * scales).reshape(deltas.shape)

def replica_grad(packed):
    activations, key_weight, key_target, norm_gain = packed
    wide = activations.astype(jnp.float32)
    inv_rms = lax.rsqrt(lax.optimization_barrier(jnp.mean(wide * wide, axis=1, keepdims=True)) + 1e-05)
    normed = (wide * inv_rms * norm_gain[None, :]).astype(jnp.bfloat16)
    keys = jnp.dot(normed, key_weight, preferred_element_type=jnp.float32)
    key_cot = ((keys - key_target.astype(jnp.float32)) / jnp.sqrt(jnp.float32(TOKENS))).astype(jnp.bfloat16)
    grouped = normed.reshape(N_FSDP, TOK_DEV, D).astype(jnp.float32)
    cot_groups = key_cot.reshape(N_FSDP, TOK_DEV, KI).astype(jnp.float32)
    partial_grad = jnp.einsum('gtd,gtk->gdk', grouped, cot_groups).astype(jnp.bfloat16)
    return lax.optimization_barrier(jnp.sum(partial_grad.astype(jnp.float32), axis=0)).astype(jnp.bfloat16)

def reference(activations, norm_gain, key_weight, key_target, replica_frag, outer_params, outer_moment):

    def accumulate(totals, frag_one):
        return (totals + decode_rows(outer_params - frag_one.astype(jnp.float32)), None)
    totals, unused = lax.scan(accumulate, jnp.zeros(outer_params.shape, jnp.float32), replica_frag)
    mean_delta = totals / jnp.float32(REPS)
    new_moment = 0.9 * outer_moment + mean_delta
    new_params = outer_params - 0.7 * (mean_delta + 0.9 * new_moment)
    fresh_frag = new_params.astype(jnp.bfloat16)
    gains = jnp.broadcast_to(norm_gain[None, :], (REPS, D))
    weight_grad = lax.map(replica_grad, (activations, key_weight, key_target, gains))
    return (new_params, new_moment, fresh_frag, weight_grad)
```

```python
import functools

import jax
import jax.numpy as jnp
from jax import lax
from jax.experimental import pallas as pl
from jax.experimental.pallas import tpu as pltpu
from jax.sharding import PartitionSpec as P

BLOCK = 128
N_Y = 4
N_X = 2
PER_STEP = 4


def y_shift(step):
    return [
        (y * N_X + x, ((y + step) % N_Y) * N_X + x) for y in range(N_Y) for x in range(N_X)
    ]


X_SWAP = [(y * N_X + x, y * N_X + 1 - x) for y in range(N_Y) for x in range(N_X)]


def send_y(block, step):
    return lax.ppermute(block, "fsdp", y_shift(step))


def power_not_below(needed):
    scale = jnp.full(needed.shape, 2.0**-30, jnp.float32)
    inverse = jnp.full(needed.shape, 2.0**30, jnp.float32)
    rest = needed
    for step in (32, 16, 8, 4, 2, 1):
        above = rest > 2.0 ** (step - 31)
        scale = jnp.where(above, scale * 2.0**step, scale)
        inverse = jnp.where(above, inverse * 2.0**-step, inverse)
        rest = jnp.where(above, rest * 2.0**-step, rest)
    return scale, inverse


def round_to_grid(magnitude):
    rest = magnitude
    spacing = jnp.full(magnitude.shape, 2.0**-9, jnp.float32)
    for step in (8, 4, 2, 1):
        above = rest >= 2.0 ** (step - 6)
        spacing = jnp.where(above, spacing * 2.0**step, spacing)
        rest = jnp.where(above, rest * 2.0**-step, rest)
    return jnp.floor(rest * 512.0 + 0.5) * spacing


def outer_kernel(replicas, frag_ref, params_ref, moment_ref, new_params_ref, new_moment_ref, fresh_ref, total):
    step = pl.program_id(0)

    @pl.when(step == 0)
    def start():
        total[...] = jnp.zeros_like(total)

    rows, cols = params_ref.shape
    blocks = cols // BLOCK
    lane = lax.broadcasted_iota(jnp.int32, (rows, BLOCK), 1)

    def delta(replica, block):
        at = pl.ds(block * BLOCK, BLOCK)
        return params_ref[:, at] - frag_ref[replica, :, at].astype(jnp.float32)

    largest = jnp.zeros((rows, BLOCK), jnp.float32)
    for replica in range(PER_STEP):
        for block in range(blocks):
            peak = jnp.max(jnp.abs(delta(replica, block)), axis=1, keepdims=True)
            largest = jnp.where(lane == replica * blocks + block, peak, largest)
    scales, inverses = power_not_below((largest + 1e-06) / 448.0)
    for block in range(blocks):
        at = pl.ds(block * BLOCK, BLOCK)
        term = total[:, at]
        for replica in range(PER_STEP):
            slot = replica * blocks + block
            diff = delta(replica, block)
            level = round_to_grid(jnp.abs(diff) * inverses[:, slot : slot + 1])
            decoded = level * scales[:, slot : slot + 1]
            term = term + jnp.where(diff < 0, -decoded, decoded)
        total[:, at] = term

    @pl.when(step == pl.num_programs(0) - 1)
    def finish():
        mean_delta = total[...] / jnp.float32(replicas)
        new_moment = 0.9 * moment_ref[...] + mean_delta
        new_params = params_ref[...] - 0.7 * (mean_delta + 0.9 * new_moment)
        new_moment_ref[...] = new_moment
        new_params_ref[...] = new_params
        fresh_ref[...] = new_params.astype(jnp.bfloat16)


def outer_step(frags, outer_params, outer_moment):
    replicas, rows, cols = frags.shape
    whole = pl.BlockSpec((rows, cols), lambda i: (0, 0))
    return pl.pallas_call(
        functools.partial(outer_kernel, replicas),
        grid=(replicas // PER_STEP,),
        in_specs=[pl.BlockSpec((PER_STEP, rows, cols), lambda i: (i, 0, 0)), whole, whole],
        out_specs=[whole, whole, whole],
        out_shape=[
            jax.ShapeDtypeStruct((rows, cols), jnp.float32),
            jax.ShapeDtypeStruct((rows, cols), jnp.float32),
            jax.ShapeDtypeStruct((rows, cols), jnp.bfloat16),
        ],
        scratch_shapes=[pltpu.VMEM((rows, cols), jnp.float32)],
        cost_estimate=pl.CostEstimate(
            flops=40 * replicas * rows * cols, bytes_accessed=3 * replicas * rows * cols, transcendentals=0
        ),
    )(frags, outer_params, outer_moment)


def per_device(
    activations, norm_gain, key_weight, key_target, replica_frag, outer_params, outer_moment
):
    place = lax.axis_index("fsdp")
    y = place // N_X
    x = place % N_X
    tokens = activations[0]
    quarter = tokens.shape[1] // N_Y
    rows = quarter // N_X
    token_count = tokens.shape[0] * lax.axis_size("fsdp")

    fragment = replica_frag[0]
    frags = lax.all_to_all(fragment, "rep", 0, 0, tiled=True)
    frags = frags.reshape(lax.axis_size("rep"), -1, fragment.shape[1])
    new_params, new_moment, fresh = outer_step(frags, outer_params, outer_moment)
    fresh_frag = lax.all_gather(fresh, "rep", axis=0, tiled=True)

    def columns(step):
        return lax.dynamic_slice(tokens, (0, lax.rem(y + step, N_Y) * quarter), (tokens.shape[0], quarter))

    weight = key_weight[0]
    held = [columns(0), send_y(columns(1), 1), send_y(columns(2), 2), send_y(columns(3), 3)]
    other = lax.ppermute(weight, "fsdp", X_SWAP)
    gain = lax.dynamic_slice(norm_gain, (y * quarter,), (quarter,))
    pair = jnp.where(
        x == 0, jnp.concatenate([weight, other]), jnp.concatenate([other, weight])
    )
    pair = (pair.astype(jnp.float32) * gain[:, None]).astype(jnp.bfloat16)
    wide = tokens.astype(jnp.float32)
    inv_rms = lax.rsqrt(jnp.mean(wide * wide, axis=1, keepdims=True) + 1e-05)
    keys = jnp.dot(held[0], pair, preferred_element_type=jnp.float32)
    for step in (1, 2, 3):
        part = jnp.dot(held[step], pair, preferred_element_type=jnp.float32)
        keys = keys + send_y(part.astype(jnp.bfloat16), N_Y - step).astype(jnp.float32)
    key_cot = (keys * inv_rms - key_target[0].astype(jnp.float32)) / jnp.sqrt(jnp.float32(token_count))
    key_cot = (key_cot * inv_rms).astype(jnp.bfloat16)
    cots = [key_cot] + [send_y(key_cot, step) for step in (1, 2, 3)]

    def grad(at):
        total = None
        for block, cot in zip(held, cots):
            part = lax.dot_general(
                lax.dynamic_slice(block, (0, at * rows), (block.shape[0], rows)),
                cot,
                (((0,), (0,)), ((), ())),
                preferred_element_type=jnp.float32,
            )
            total = part if total is None else total + part
        return total

    theirs = lax.ppermute(grad(1 - x).astype(jnp.bfloat16), "fsdp", X_SWAP)
    own_gain = lax.dynamic_slice(norm_gain, (place * rows,), (rows,))
    weight_grad = ((grad(x) + theirs.astype(jnp.float32)) * own_gain[:, None]).astype(jnp.bfloat16)
    return (new_params, new_moment, fresh_frag, weight_grad[None])


def solution(mesh):
    placed = (
        P("rep", "fsdp", None),
        P(),
        P("rep", "fsdp", None),
        P("rep", "fsdp", None),
        P("rep", "fsdp", None),
        P(("fsdp", "rep"), None),
        P(("fsdp", "rep"), None),
    )
    return jax.shard_map(
        per_device,
        mesh=mesh,
        in_specs=placed,
        out_specs=(
            P(("fsdp", "rep"), None),
            P(("fsdp", "rep"), None),
            P("fsdp", None),
            P("rep", "fsdp", None),
        ),
        check_vma=False,
    )
```

```python
import functools

import jax
import jax.numpy as jnp
from jax import lax
from jax.experimental import pallas as pl
from jax.experimental.pallas import tpu as pltpu
from jax.sharding import PartitionSpec as P

BLOCK = 128
N_Y = 4
N_X = 2
PER_STEP = 8
N_CORE = 2
ANY = pl.BlockSpec(memory_space=pl.ANY)
HBM = pl.BlockSpec(memory_space=pltpu.HBM)
VMEM = pl.BlockSpec(memory_space=pltpu.VMEM)
SMEM = pl.BlockSpec(memory_space=pltpu.SMEM)
PARAMS = pltpu.CompilerParams(vmem_limit_bytes=24 * 2**20)
COST = pl.CostEstimate(flops=10**12, bytes_accessed=10**9, transcendentals=10**9)
SHORT = pl.CostEstimate(flops=2 * 10**10, bytes_accessed=10**6, transcendentals=0)


def in_hbm(array):
    return pltpu.with_memory_space_constraint(array, pltpu.HBM)


def y_shift(step):
    return [
        (y * N_X + x, ((y + step) % N_Y) * N_X + x) for y in range(N_Y) for x in range(N_X)
    ]


X_SWAP = [(y * N_X + x, y * N_X + 1 - x) for y in range(N_Y) for x in range(N_X)]


def send_y(block, step):
    return lax.ppermute(block, "fsdp", y_shift(step))


def power_not_below(needed):
    scale = jnp.full(needed.shape, 2.0**-30, jnp.float32)
    inverse = jnp.full(needed.shape, 2.0**30, jnp.float32)
    rest = needed
    for step in (32, 16, 8, 4, 2, 1):
        above = rest > 2.0 ** (step - 31)
        scale = jnp.where(above, scale * 2.0**step, scale)
        inverse = jnp.where(above, inverse * 2.0**-step, inverse)
        rest = jnp.where(above, rest * 2.0**-step, rest)
    return scale, inverse


def grid_spacing(magnitude):
    whole = jnp.maximum((magnitude * 64.0).astype(jnp.int32), 1)
    power = 31 - lax.clz(whole)
    one = jnp.ones_like(whole)
    spacing = lax.shift_left(one, power).astype(jnp.float32)
    inverse = lax.shift_left(one, 15 - power).astype(jnp.float32) * 2.0**-15
    return spacing, inverse


def outer_kernel(
    replicas, frag_ref, params_ref, moment_ref, *refs
):
    new_params_ref, new_moment_ref, fresh_ref, total = refs[-4:]
    step = pl.program_id(0)

    @pl.when(step == 0)
    def start():
        total[...] = jnp.zeros_like(total)

    rows, cols = params_ref.shape
    blocks = cols // BLOCK
    lane = lax.broadcasted_iota(jnp.int32, (rows, BLOCK), 1)

    def delta(replica, block):
        at = pl.ds(block * BLOCK, BLOCK)
        return params_ref[:, at] - frag_ref[replica, :, at].astype(jnp.float32)

    largest = jnp.zeros((rows, BLOCK), jnp.float32)
    for replica in range(PER_STEP):
        for block in range(blocks):
            peak = jnp.max(jnp.abs(delta(replica, block)), axis=1, keepdims=True)
            largest = jnp.where(lane == replica * blocks + block, peak, largest)
    scales, inverses = power_not_below((largest + 1e-06) / 448.0)
    for block in range(blocks):
        at = pl.ds(block * BLOCK, BLOCK)
        term = total[:, at]
        for replica in range(PER_STEP):
            slot = replica * blocks + block
            diff = delta(replica, block)
            magnitude = jnp.abs(diff) * inverses[:, slot : slot + 1]
            spacing, inverse = grid_spacing(magnitude)
            level = jnp.floor(magnitude * (inverse * 512.0) + 0.5)
            decoded = level * (spacing * (scales[:, slot : slot + 1] * 2.0**-9))
            term = term + jnp.where(diff < 0, -decoded, decoded)
        total[:, at] = term

    @pl.when(step == pl.num_programs(0) - 1)
    def finish():
        mean_delta = total[...] / jnp.float32(replicas)
        new_moment = 0.9 * moment_ref[...] + mean_delta
        new_params = params_ref[...] - 0.7 * (mean_delta + 0.9 * new_moment)
        new_moment_ref[...] = new_moment
        new_params_ref[...] = new_params
        fresh_ref[...] = new_params.astype(jnp.bfloat16)


def outer_step(frags, outer_params, outer_moment, *after):
    replicas, rows, cols = frags.shape
    whole = pl.BlockSpec((rows, cols), lambda i: (0, 0))
    return pl.pallas_call(
        functools.partial(outer_kernel, replicas),
        grid=(replicas // PER_STEP,),
        in_specs=[pl.BlockSpec((PER_STEP, rows, cols), lambda i: (i, 0, 0)), whole, whole] + [ANY] * len(after),
        out_specs=[whole, whole, whole],
        out_shape=[
            jax.ShapeDtypeStruct((rows, cols), jnp.float32),
            jax.ShapeDtypeStruct((rows, cols), jnp.float32),
            jax.ShapeDtypeStruct((rows, cols), jnp.bfloat16),
        ],
        scratch_shapes=[pltpu.VMEM((rows, cols), jnp.float32)],
        compiler_params=PARAMS,
        cost_estimate=COST,
        name="outer",
    )(frags, outer_params, outer_moment, *after)


def spread_kernel(source_ref, *refs):
    target_ref = refs[-1]
    for copy in range(target_ref.shape[0]):
        target_ref[copy] = source_ref[...]


def spread(source, copies, *after):
    shape = (copies,) + source.shape
    return pl.pallas_call(
        spread_kernel,
        in_specs=[VMEM] + [ANY] * len(after),
        out_specs=VMEM,
        out_shape=pltpu.VMEM(shape, source.dtype),
        compiler_params=PARAMS,
        cost_estimate=COST,
        name="spread",
    )(source, *after)


PIECES = 4


def merge_kernel(core_ref, mine_ref, theirs_ref, out_ref, held, in_sems, out_sems):
    core = core_ref[0]
    chips = held.shape[1] // PIECES
    reads, writes = [], []
    for piece in range(PIECES):
        at = pl.ds(piece * chips, chips)
        for which, (source, slot) in enumerate(((mine_ref, core), (theirs_ref, 1 - core))):
            sem = which * PIECES + piece
            reads.append(pltpu.make_async_copy(source.at[at], held.at[which, at], in_sems.at[sem]))
            writes.append(
                pltpu.make_async_copy(held.at[which, at], out_ref.at[at, slot], out_sems.at[sem])
            )
    for read in reads:
        read.start()
    for read, write in zip(reads, writes):
        read.wait()
        write.start()
    for write in writes:
        write.wait()


def merge_cores(core, mine, theirs):
    chips, rows, cols = mine.shape
    return pl.pallas_call(
        merge_kernel,
        in_specs=[SMEM, HBM, HBM],
        out_specs=HBM,
        out_shape=jax.ShapeDtypeStruct((chips, N_CORE, rows, cols), mine.dtype),
        scratch_shapes=[
            pltpu.VMEM((N_CORE,) + mine.shape, mine.dtype),
            pltpu.SemaphoreType.DMA((N_CORE * PIECES,)),
            pltpu.SemaphoreType.DMA((N_CORE * PIECES,)),
        ],
        compiler_params=PARAMS,
        name="merge",
    )(core.reshape(1), in_hbm(mine), in_hbm(theirs))


def cut_kernel(count, kept, at_ref, source_ref, *refs):
    targets, (buffer, in_sems, out_sems) = refs[-3 - count : -3], refs[-3:]
    width = buffer.shape[3]
    reads, writes = [], []
    for which in range(count):
        for half in range(N_X):
            columns = pl.ds(pl.multiple_of((at_ref[which] * N_X + half) * width, width), width)
            slot = which * N_X + half
            held = buffer.at[which, half] if which < count - kept else targets[which].at[half]
            reads.append(pltpu.make_async_copy(source_ref.at[:, columns], held, in_sems.at[slot]))
            if which < count - kept:
                writes.append(pltpu.make_async_copy(held, targets[which].at[half], out_sems.at[slot]))
    for read in reads:
        read.start()
    for slot, read in enumerate(reads):
        read.wait()
        if slot < len(writes):
            writes[slot].start()
    for write in writes:
        write.wait()


def cut_columns(tokens, places, width, kept, *after):
    rows = tokens.shape[0]
    count = len(places)
    moved = count - kept
    shape = (N_X, rows, width // N_X)
    return pl.pallas_call(
        functools.partial(cut_kernel, count, kept),
        in_specs=[SMEM, HBM] + [ANY] * len(after),
        out_specs=[HBM] * moved + [VMEM] * kept,
        out_shape=[jax.ShapeDtypeStruct(shape, tokens.dtype)] * moved + [pltpu.VMEM(shape, tokens.dtype)] * kept,
        scratch_shapes=[
            pltpu.VMEM((moved,) + shape, tokens.dtype),
            pltpu.SemaphoreType.DMA((count * N_X,)),
            pltpu.SemaphoreType.DMA((moved * N_X,)),
        ],
        compiler_params=PARAMS,
        cost_estimate=COST,
        name="cut",
    )(jnp.stack(places), in_hbm(tokens), *(in_hbm(one) for one in after))


def behind_kernel(source_ref, *refs):
    target_ref, buffer, in_sems, out_sems = refs[-4:]
    rows = source_ref.shape[0] // 4
    reads, writes = [], []
    for part in range(4):
        at = pl.ds(part * rows, rows)
        reads.append(pltpu.make_async_copy(source_ref.at[at], buffer.at[at], in_sems.at[part]))
        writes.append(pltpu.make_async_copy(buffer.at[at], target_ref.at[at], out_sems.at[part]))
    for read in reads:
        read.start()
    for read, write in zip(reads, writes):
        read.wait()
        write.start()
    for write in writes:
        write.wait()


def behind(source, *after):
    return pl.pallas_call(
        behind_kernel,
        in_specs=[ANY] * (1 + len(after)),
        out_specs=ANY,
        out_shape=jax.ShapeDtypeStruct(source.shape, source.dtype),
        scratch_shapes=[
            pltpu.VMEM(source.shape, source.dtype),
            pltpu.SemaphoreType.DMA((4,)),
            pltpu.SemaphoreType.DMA((4,)),
        ],
        compiler_params=PARAMS,
        cost_estimate=COST,
        name="behind",
    )(in_hbm(source), *(in_hbm(one) for one in after))


def pair_kernel(x_ref, weight_ref, other_ref, gain_ref, pair_ref):
    x = x_ref[0]
    width = weight_ref.shape[1]
    for which, source in enumerate((weight_ref, other_ref)):
        at = x if which == 0 else 1 - x
        factor = jnp.concatenate([gain_ref[at]] * (width // BLOCK), axis=1)
        pair_ref[at] = (source[...].astype(jnp.float32) * factor).astype(jnp.bfloat16)


def scaled_pair(x, weight, other, gain):
    return pl.pallas_call(
        pair_kernel,
        in_specs=[SMEM] + [VMEM] * 3,
        out_specs=VMEM,
        out_shape=pltpu.VMEM((N_X,) + weight.shape, weight.dtype),
        compiler_params=PARAMS,
        cost_estimate=COST,
        name="pair",
    )(x.reshape(1), weight, other, gain)


def own_kernel(token_count, tokens_ref, block_ref, weight_ref, key_target_ref, base_ref, factor_ref):
    wide = tokens_ref[...].astype(jnp.float32)
    inv_rms = lax.rsqrt(jnp.mean(wide * wide, axis=1, keepdims=True) + 1e-05)
    rows = tokens_ref.shape[0]
    at = pl.ds(pl.multiple_of(pl.program_id(0) * rows, rows), rows)
    keys = sum(
        jnp.dot(block_ref[half, at, :], weight_ref[half], preferred_element_type=jnp.float32)
        for half in range(N_X)
    )
    root = jnp.sqrt(jnp.float32(token_count))
    base_ref[...] = (keys * inv_rms - key_target_ref[...].astype(jnp.float32)) / root * inv_rms
    factor_ref[...] = jnp.broadcast_to(inv_rms * inv_rms / root, factor_ref.shape)


def own_part(tokens, block, weight, key_target, token_count):
    rows, depth = tokens.shape
    width = weight.shape[2]
    part = rows // 3
    return pl.pallas_call(
        functools.partial(own_kernel, token_count),
        grid=(3,),
        in_specs=[
            pl.BlockSpec((part, depth), lambda i: (i, 0)),
            VMEM,
            VMEM,
            pl.BlockSpec((part, width), lambda i: (i, 0)),
        ],
        out_specs=[pl.BlockSpec((part, wide), lambda i: (i, 0)) for wide in (width, BLOCK)],
        out_shape=[jax.ShapeDtypeStruct((rows, wide), jnp.float32) for wide in (width, BLOCK)],
        compiler_params=PARAMS,
        cost_estimate=COST,
        name="own",
    )(in_hbm(tokens), block, weight, in_hbm(key_target))


SPLIT = 4


def part_kernel(block_ref, weight_ref, *refs):
    part_ref, kept_ref, sems = refs[-3:]
    rows = kept_ref.shape[1] // SPLIT
    reads = []
    for half in range(N_X):
        for piece in range(SPLIT):
            at = pl.ds(piece * rows, rows)
            reads.append(
                pltpu.make_async_copy(
                    block_ref.at[half, at], kept_ref.at[half, at], sems.at[half * SPLIT + piece]
                )
            )
    for read in reads:
        read.start()
    total = None
    for half in range(N_X):
        for read in reads[half * SPLIT : (half + 1) * SPLIT]:
            read.wait()
        term = jnp.dot(kept_ref[half], weight_ref[half], preferred_element_type=jnp.float32)
        total = term if total is None else total + term
    part_ref[...] = total.astype(jnp.bfloat16)


def key_part(block, weight, *after):
    return pl.pallas_call(
        part_kernel,
        in_specs=[HBM, VMEM] + [ANY] * len(after),
        out_specs=VMEM,
        out_shape=jax.ShapeDtypeStruct((block.shape[1], weight.shape[2]), jnp.bfloat16),
        scratch_shapes=[pltpu.VMEM(block.shape, block.dtype), pltpu.SemaphoreType.DMA((N_X * SPLIT,))],
        compiler_params=PARAMS,
        cost_estimate=COST,
        name="part",
    )(in_hbm(block), weight, *after)


HALVES = 2


def cot_kernel(*refs):
    sources, halves, held, sems = refs[:5], refs[-6 - HALVES : -6], refs[-6:-1], refs[-1]
    reads = [pltpu.make_async_copy(source, target, sems.at[i]) for i, (source, target) in enumerate(zip(sources, held))]
    for read in reads:
        read.start()
    for read in reads:
        read.wait()
    base, factor, first, second, third = held
    width = halves[0].shape[0]
    wide = jnp.concatenate([factor[...]] * (width // BLOCK), axis=1)
    for half, out_ref in enumerate(halves):
        at = pl.ds(half * width, width)
        others = (
            first[:, at].astype(jnp.float32)
            + second[:, at].astype(jnp.float32)
            + third[:, at].astype(jnp.float32)
        )
        out_ref[...] = (base[:, at] + wide * others).T.astype(jnp.bfloat16)


def cotangent(base, factor, parts, *after):
    rows, width = base.shape
    sources = [base, factor, *parts]
    return pl.pallas_call(
        cot_kernel,
        in_specs=[HBM] * 5 + [ANY] * len(after),
        out_specs=[VMEM] * HALVES,
        out_shape=[jax.ShapeDtypeStruct((width // HALVES, rows), jnp.bfloat16)] * HALVES,
        scratch_shapes=[pltpu.VMEM(one.shape, one.dtype) for one in sources] + [pltpu.SemaphoreType.DMA((5,))],
        compiler_params=PARAMS,
        cost_estimate=COST,
        name="cot",
    )(*(in_hbm(one) for one in sources), *after)


def add_kernel(half, own_ref, theirs_ref, *refs):
    out_ref, held, total, in_sems, out_sems = refs[-5:]
    rows, width = theirs_ref.shape
    piece = rows // PIECES
    columns = pl.ds(half * width, width)
    reads, writes = [], []
    for which in range(PIECES):
        at = pl.ds(which * piece, piece)
        reads.append(pltpu.make_async_copy(theirs_ref.at[at], held.at[at], in_sems.at[which]))
        writes.append(pltpu.make_async_copy(total.at[at], out_ref.at[at, columns], out_sems.at[which]))
    for read in reads:
        read.start()
    for which in range(PIECES):
        at = pl.ds(which * piece, piece)
        reads[which].wait()
        total[at, :] = (own_ref[at, columns] + held[at, :].astype(jnp.float32)).astype(jnp.bfloat16)
        writes[which].start()
    for write in writes:
        write.wait()


def add_half(half, own, theirs, before, *after):
    rows, width = theirs.shape
    return pl.pallas_call(
        functools.partial(add_kernel, half),
        in_specs=[VMEM, HBM] + [HBM] * (before is not None) + [ANY] * len(after),
        out_specs=HBM,
        out_shape=jax.ShapeDtypeStruct(own.shape, jnp.bfloat16),
        input_output_aliases={} if before is None else {2: 0},
        scratch_shapes=[
            pltpu.VMEM(theirs.shape, jnp.bfloat16),
            pltpu.VMEM(theirs.shape, jnp.bfloat16),
            pltpu.SemaphoreType.DMA((PIECES,)),
            pltpu.SemaphoreType.DMA((PIECES,)),
        ],
        compiler_params=PARAMS,
        name="add",
    )(own, in_hbm(theirs), *(() if before is None else (before,)), *(in_hbm(one) for one in after))


TILES = 2


def load_kernel(count, *refs):
    sources, gain_ref, targets, gain, sems = refs[:count], refs[count], refs[-2 - count : -2], refs[-2], refs[-1]
    reads = [pltpu.make_async_copy(gain_ref, gain, sems.at[2 * count])]
    for which in range(count):
        for half in range(N_X):
            reads.append(
                pltpu.make_async_copy(
                    sources[which].at[half], targets[which].at[half], sems.at[which * N_X + half]
                )
            )
    for read in reads:
        read.start()
    for read in reads:
        read.wait()


def load_blocks(blocks, gain, *after):
    count = len(blocks)
    kept = [pltpu.VMEM(one.shape, one.dtype) for one in (*blocks, gain)]
    *loaded, gain = pl.pallas_call(
        functools.partial(load_kernel, count),
        in_specs=[HBM] * (count + 1) + [ANY] * len(after),
        out_specs=[VMEM] * (count + 1),
        out_shape=kept,
        scratch_shapes=[pltpu.SemaphoreType.DMA((2 * count + 1,))],
        compiler_params=PARAMS,
        name="load",
    )(*(in_hbm(one) for one in (*blocks, gain)), *after)
    return loaded, gain


def grad_kernel(count, half_ref, *refs):
    blocks, gain_ref, cots, out_ref = refs[:count], refs[count], refs[count + 1 : -1], refs[-1]
    half = half_ref[0]
    width = cots[0].shape[0]
    tile = out_ref.shape[0] // TILES
    for part in range(TILES):
        at = pl.ds(part * tile, tile)
        block = jnp.concatenate([ref[half, :, at] for ref in blocks], axis=0)
        factor = jnp.concatenate([gain_ref[half, at, :]] * (width // BLOCK), axis=1)
        for group in range(len(cots) // count):
            cot = jnp.concatenate([ref[...] for ref in cots[group * count : (group + 1) * count]], axis=1)
            total = jnp.dot(cot, block, preferred_element_type=jnp.float32).T * factor
            out_ref[at, pl.ds(group * width, width)] = total.astype(out_ref.dtype)


def grad_rows(blocks, half, cots, gain, out, cost):
    count = len(blocks)
    return pl.pallas_call(
        functools.partial(grad_kernel, count),
        in_specs=[SMEM] + [VMEM] * (count + 1 + len(cots)),
        out_specs=VMEM,
        out_shape=out,
        compiler_params=PARAMS,
        cost_estimate=cost,
        name="grad",
    )(half.reshape(1), *blocks, gain, *cots)


def per_device(
    activations, norm_gain, key_weight, key_target, replica_frag, outer_params, outer_moment
):
    place = lax.axis_index("fsdp")
    y = place // N_X
    x = place % N_X
    tokens = activations[0]
    quarter = tokens.shape[1] // N_Y
    rows = quarter // N_X
    token_count = tokens.shape[0] * lax.axis_size("fsdp")

    places = {step: lax.rem(y + step, N_Y) for step in (2, 1, 3)}
    sent = {}
    (sent[2],) = cut_columns(tokens, [places[2]], quarter, 0)
    held = {2: send_y(sent[2], 2)}

    fragment = behind(replica_frag[0], sent[2])
    frags = lax.all_to_all(fragment, "rep", 0, 0, tiled=True)
    frags = frags.reshape(lax.axis_size("rep"), -1, fragment.shape[1])

    sent[1], sent[3], own = cut_columns(
        tokens, [places[1], places[3], y], quarter, 0, fragment
    )
    held[1], held[3] = send_y(sent[1], 1), send_y(sent[3], 3)
    weight = key_weight[0]
    other = lax.ppermute(weight, "fsdp", X_SWAP)

    gain = lax.dynamic_slice(norm_gain, (y * quarter,), (quarter,))
    wide_gain = jnp.broadcast_to(gain.reshape(N_X, rows, 1), (N_X, rows, BLOCK))
    pair = scaled_pair(x, weight, other, wide_gain)
    base, factor = own_part(tokens, own, pair, key_target[0], token_count)
    parts = {}
    parts[2] = key_part(held[2], pair, base)
    new_params, new_moment, fresh = outer_step(frags, outer_params, outer_moment, parts[2])
    parts[1] = key_part(held[1], pair, fresh)
    parts[3] = key_part(held[3], pair, parts[1])
    chips = lax.axis_size("rep") // N_CORE
    many = spread(fresh, chips, parts[3])
    others = [send_y(parts[step], N_Y - step) for step in (2, 1, 3)]
    cot = cotangent(base, factor, others, many)
    cots = [[part] + [send_y(part, step) for step in (2, 1, 3)] for part in cot]

    cores = [[chip * N_CORE + core for chip in range(chips)] for core in range(N_CORE)]
    own_rows, cols = fresh.shape
    mine = lax.all_to_all(
        many.reshape(chips * own_rows, cols),
        "rep",
        0,
        0,
        axis_index_groups=cores,
        tiled=True,
    ).reshape(chips, own_rows, cols)
    theirs = lax.ppermute(mine, "rep", [(i, i ^ 1) for i in range(chips * N_CORE)])
    fresh_frag = merge_cores(lax.axis_index("rep") % N_CORE, mine, theirs).reshape(-1, cols)

    blocks, wide_gain = load_blocks([own, held[2], held[1], held[3]], wide_gain, cot[0])
    width = cot[0].shape[0]
    theirs = []
    for half in range(HALVES):
        out = jax.ShapeDtypeStruct((rows, width), jnp.bfloat16)
        part = grad_rows(blocks, 1 - x, cots[half], wide_gain, out, None)
        theirs.append(lax.ppermute(part, "fsdp", X_SWAP))
    out = pltpu.VMEM((rows, HALVES * width), jnp.float32)
    mine_grad = grad_rows(blocks, x, cots[0] + cots[1], wide_gain, out, SHORT)
    weight_grad = add_half(0, mine_grad, theirs[0], None)
    weight_grad = add_half(1, mine_grad, theirs[1], weight_grad, fresh_frag)
    return (new_params, new_moment, fresh_frag, weight_grad[None])


def solution(mesh):
    placed = (
        P("rep", "fsdp", None),
        P(),
        P("rep", "fsdp", None),
        P("rep", "fsdp", None),
        P("rep", "fsdp", None),
        P(("fsdp", "rep"), None),
        P(("fsdp", "rep"), None),
    )
    return jax.shard_map(
        per_device,
        mesh=mesh,
        in_specs=placed,
        out_specs=(
            P(("fsdp", "rep"), None),
            P(("fsdp", "rep"), None),
            P("fsdp", None),
            P("rep", "fsdp", None),
        ),
        check_vma=False,
    )
```

```python
import functools

import jax
import jax.numpy as jnp
from jax import lax
from jax.experimental import pallas as pl
from jax.experimental.pallas import tpu as pltpu
from jax.sharding import PartitionSpec as P

BLOCK = 128
N_Y = 4
N_X = 2
PER_STEP = 8
N_CORE = 2
ANY = pl.BlockSpec(memory_space=pl.ANY)
HBM = pl.BlockSpec(memory_space=pltpu.HBM)
VMEM = pl.BlockSpec(memory_space=pltpu.VMEM)
SMEM = pl.BlockSpec(memory_space=pltpu.SMEM)
PARAMS = pltpu.CompilerParams(vmem_limit_bytes=24 * 2**20)
COST = pl.CostEstimate(flops=10**12, bytes_accessed=10**9, transcendentals=10**9)
SHORT = pl.CostEstimate(flops=2 * 10**10, bytes_accessed=10**6, transcendentals=0)


def in_hbm(array):
    return pltpu.with_memory_space_constraint(array, pltpu.HBM)


def y_shift(step):
    return [
        (y * N_X + x, ((y + step) % N_Y) * N_X + x) for y in range(N_Y) for x in range(N_X)
    ]


X_SWAP = [(y * N_X + x, y * N_X + 1 - x) for y in range(N_Y) for x in range(N_X)]


def send_y(block, step):
    return lax.ppermute(block, "fsdp", y_shift(step))


def power_not_below(needed):
    scale = jnp.full(needed.shape, 2.0**-30, jnp.float32)
    inverse = jnp.full(needed.shape, 2.0**30, jnp.float32)
    rest = needed
    for step in (32, 16, 8, 4, 2, 1):
        above = rest > 2.0 ** (step - 31)
        scale = jnp.where(above, scale * 2.0**step, scale)
        inverse = jnp.where(above, inverse * 2.0**-step, inverse)
        rest = jnp.where(above, rest * 2.0**-step, rest)
    return scale, inverse


def grid_spacing(magnitude):
    whole = jnp.maximum((magnitude * 64.0).astype(jnp.int32), 1)
    power = 31 - lax.clz(whole)
    one = jnp.ones_like(whole)
    spacing = lax.shift_left(one, power).astype(jnp.float32)
    inverse = lax.shift_left(one, 15 - power).astype(jnp.float32) * 2.0**-15
    return spacing, inverse


def outer_kernel(
    replicas, frag_ref, params_ref, moment_ref, *refs
):
    new_params_ref, new_moment_ref, fresh_ref, total = refs[-4:]
    step = pl.program_id(0)

    @pl.when(step == 0)
    def start():
        total[...] = jnp.zeros_like(total)

    rows, cols = params_ref.shape
    blocks = cols // BLOCK
    lane = lax.broadcasted_iota(jnp.int32, (rows, BLOCK), 1)

    def delta(replica, block):
        at = pl.ds(block * BLOCK, BLOCK)
        return params_ref[:, at] - frag_ref[replica, :, at].astype(jnp.float32)

    largest = jnp.zeros((rows, BLOCK), jnp.float32)
    for replica in range(PER_STEP):
        for block in range(blocks):
            peak = jnp.max(jnp.abs(delta(replica, block)), axis=1, keepdims=True)
            largest = jnp.where(lane == replica * blocks + block, peak, largest)
    scales, inverses = power_not_below((largest + 1e-06) / 448.0)
    for block in range(blocks):
        at = pl.ds(block * BLOCK, BLOCK)
        term = total[:, at]
        for replica in range(PER_STEP):
            slot = replica * blocks + block
            diff = delta(replica, block)
            magnitude = jnp.abs(diff) * inverses[:, slot : slot + 1]
            spacing, inverse = grid_spacing(magnitude)
            level = jnp.floor(magnitude * (inverse * 512.0) + 0.5)
            decoded = level * (spacing * (scales[:, slot : slot + 1] * 2.0**-9))
            term = term + jnp.where(diff < 0, -decoded, decoded)
        total[:, at] = term

    @pl.when(step == pl.num_programs(0) - 1)
    def finish():
        mean_delta = total[...] / jnp.float32(replicas)
        new_moment = 0.9 * moment_ref[...] + mean_delta
        new_params = params_ref[...] - 0.7 * (mean_delta + 0.9 * new_moment)
        new_moment_ref[...] = new_moment
        new_params_ref[...] = new_params
        fresh_ref[...] = new_params.astype(jnp.bfloat16)


def outer_step(frags, outer_params, outer_moment, *after):
    replicas, rows, cols = frags.shape
    whole = pl.BlockSpec((rows, cols), lambda i: (0, 0))
    return pl.pallas_call(
        functools.partial(outer_kernel, replicas),
        grid=(replicas // PER_STEP,),
        in_specs=[pl.BlockSpec((PER_STEP, rows, cols), lambda i: (i, 0, 0)), whole, whole] + [ANY] * len(after),
        out_specs=[whole, whole, whole],
        out_shape=[
            jax.ShapeDtypeStruct((rows, cols), jnp.float32),
            jax.ShapeDtypeStruct((rows, cols), jnp.float32),
            jax.ShapeDtypeStruct((rows, cols), jnp.bfloat16),
        ],
        scratch_shapes=[pltpu.VMEM((rows, cols), jnp.float32)],
        compiler_params=PARAMS,
        cost_estimate=COST,
        name="outer",
    )(frags, outer_params, outer_moment, *after)


def spread_kernel(source_ref, *refs):
    target_ref = refs[-1]
    for copy in range(target_ref.shape[0]):
        target_ref[copy] = source_ref[...]


def spread(source, copies, *after):
    shape = (copies,) + source.shape
    return pl.pallas_call(
        spread_kernel,
        in_specs=[VMEM] + [ANY] * len(after),
        out_specs=VMEM,
        out_shape=pltpu.VMEM(shape, source.dtype),
        compiler_params=PARAMS,
        cost_estimate=COST,
        name="spread",
    )(source, *after)


PIECES = 4


def merge_kernel(core_ref, mine_ref, theirs_ref, out_ref, held, in_sems, out_sems):
    core = core_ref[0]
    chips = held.shape[1] // PIECES
    reads, writes = [], []
    for piece in range(PIECES):
        at = pl.ds(piece * chips, chips)
        for which, (source, slot) in enumerate(((mine_ref, core), (theirs_ref, 1 - core))):
            sem = which * PIECES + piece
            reads.append(pltpu.make_async_copy(source.at[at], held.at[which, at], in_sems.at[sem]))
            writes.append(
                pltpu.make_async_copy(held.at[which, at], out_ref.at[at, slot], out_sems.at[sem])
            )
    for read in reads:
        read.start()
    for read, write in zip(reads, writes):
        read.wait()
        write.start()
    for write in writes:
        write.wait()


def merge_cores(core, mine, theirs):
    chips, rows, cols = mine.shape
    return pl.pallas_call(
        merge_kernel,
        in_specs=[SMEM, ANY, ANY],
        out_specs=HBM,
        out_shape=jax.ShapeDtypeStruct((chips, N_CORE, rows, cols), mine.dtype),
        scratch_shapes=[
            pltpu.VMEM((N_CORE,) + mine.shape, mine.dtype),
            pltpu.SemaphoreType.DMA((N_CORE * PIECES,)),
            pltpu.SemaphoreType.DMA((N_CORE * PIECES,)),
        ],
        compiler_params=PARAMS,
        name="merge",
    )(core.reshape(1), mine, theirs)


def cut_kernel(count, kept, at_ref, source_ref, *refs):
    targets, (buffer, in_sems, out_sems) = refs[-3 - count : -3], refs[-3:]
    width = buffer.shape[3]
    reads, writes = [], []
    for which in range(count):
        for half in range(N_X):
            columns = pl.ds(pl.multiple_of((at_ref[which] * N_X + half) * width, width), width)
            slot = which * N_X + half
            held = buffer.at[which, half] if which < count - kept else targets[which].at[half]
            reads.append(pltpu.make_async_copy(source_ref.at[:, columns], held, in_sems.at[slot]))
            if which < count - kept:
                writes.append(pltpu.make_async_copy(held, targets[which].at[half], out_sems.at[slot]))
    for read in reads:
        read.start()
    for slot, read in enumerate(reads):
        read.wait()
        if slot < len(writes):
            writes[slot].start()
    for write in writes:
        write.wait()


def cut_columns(tokens, places, width, kept, *after):
    rows = tokens.shape[0]
    count = len(places)
    moved = count - kept
    shape = (N_X, rows, width // N_X)
    return pl.pallas_call(
        functools.partial(cut_kernel, count, kept),
        in_specs=[SMEM, HBM] + [ANY] * len(after),
        out_specs=[HBM] * moved + [VMEM] * kept,
        out_shape=[jax.ShapeDtypeStruct(shape, tokens.dtype)] * moved + [pltpu.VMEM(shape, tokens.dtype)] * kept,
        scratch_shapes=[
            pltpu.VMEM((moved,) + shape, tokens.dtype),
            pltpu.SemaphoreType.DMA((count * N_X,)),
            pltpu.SemaphoreType.DMA((moved * N_X,)),
        ],
        compiler_params=PARAMS,
        cost_estimate=COST,
        name="cut",
    )(jnp.stack(places), in_hbm(tokens), *(in_hbm(one) for one in after))


def behind_kernel(count, *refs):
    sources, refs = refs[:count], refs[-2 * count - 2 :]
    targets, buffers, (in_sems, out_sems) = refs[:count], refs[count : 2 * count], refs[2 * count :]
    reads, writes = [], []
    for which in range(count):
        rows = sources[which].shape[0] // PIECES
        for piece in range(PIECES):
            at = pl.ds(piece * rows, rows)
            held = buffers[which].at[at]
            slot = which * PIECES + piece
            reads.append(pltpu.make_async_copy(sources[which].at[at], held, in_sems.at[slot]))
            writes.append(pltpu.make_async_copy(held, targets[which].at[at], out_sems.at[slot]))
    for read in reads:
        read.start()
    for read, write in zip(reads, writes):
        read.wait()
        write.start()
    for write in writes:
        write.wait()


def behind(sources, *after):
    count = len(sources)
    return pl.pallas_call(
        functools.partial(behind_kernel, count),
        in_specs=[HBM] * count + [ANY] * len(after),
        out_specs=[HBM] * count,
        out_shape=[jax.ShapeDtypeStruct(one.shape, one.dtype) for one in sources],
        scratch_shapes=[pltpu.VMEM(one.shape, one.dtype) for one in sources]
        + [pltpu.SemaphoreType.DMA((count * PIECES,))] * 2,
        compiler_params=PARAMS,
        cost_estimate=COST,
        name="behind",
    )(*(in_hbm(one) for one in sources), *(in_hbm(one) for one in after))


def pair_kernel(x_ref, weight_ref, other_ref, gain_ref, pair_ref):
    x = x_ref[0]
    width = weight_ref.shape[1]
    for which, source in enumerate((weight_ref, other_ref)):
        at = x if which == 0 else 1 - x
        factor = jnp.concatenate([gain_ref[at]] * (width // BLOCK), axis=1)
        pair_ref[at] = (source[...].astype(jnp.float32) * factor).astype(jnp.bfloat16)


def scaled_pair(x, weight, other, gain):
    return pl.pallas_call(
        pair_kernel,
        in_specs=[SMEM] + [VMEM] * 3,
        out_specs=VMEM,
        out_shape=pltpu.VMEM((N_X,) + weight.shape, weight.dtype),
        compiler_params=PARAMS,
        cost_estimate=COST,
        name="pair",
    )(x.reshape(1), weight, other, gain)


def own_kernel(token_count, tokens_ref, block_ref, weight_ref, key_target_ref, base_ref, factor_ref):
    wide = tokens_ref[...].astype(jnp.float32)
    inv_rms = lax.rsqrt(jnp.mean(wide * wide, axis=1, keepdims=True) + 1e-05)
    rows = tokens_ref.shape[0]
    at = pl.ds(pl.multiple_of(pl.program_id(0) * rows, rows), rows)
    keys = sum(
        jnp.dot(block_ref[half, at, :], weight_ref[half], preferred_element_type=jnp.float32)
        for half in range(N_X)
    )
    root = jnp.sqrt(jnp.float32(token_count))
    base_ref[...] = (keys * inv_rms - key_target_ref[...].astype(jnp.float32)) / root * inv_rms
    factor_ref[...] = jnp.broadcast_to(inv_rms * inv_rms / root, factor_ref.shape)


def own_part(tokens, block, weight, key_target, token_count):
    rows, depth = tokens.shape
    width = weight.shape[2]
    part = rows // 3
    return pl.pallas_call(
        functools.partial(own_kernel, token_count),
        grid=(3,),
        in_specs=[
            pl.BlockSpec((part, depth), lambda i: (i, 0)),
            VMEM,
            VMEM,
            pl.BlockSpec((part, width), lambda i: (i, 0)),
        ],
        out_specs=[pl.BlockSpec((part, wide), lambda i: (i, 0)) for wide in (width, BLOCK)],
        out_shape=[jax.ShapeDtypeStruct((rows, wide), jnp.float32) for wide in (width, BLOCK)],
        compiler_params=PARAMS,
        cost_estimate=COST,
        name="own",
    )(in_hbm(tokens), block, weight, in_hbm(key_target))


SPLIT = 4


def part_kernel(count, *refs):
    blocks, weight_ref = refs[:count], refs[count]
    parts, (held, sems) = refs[-2 - count : -2], refs[-2:]
    rows = held.shape[2] // SPLIT
    reads = []
    for which in range(count):
        for half in range(N_X):
            for piece in range(SPLIT):
                at = pl.ds(piece * rows, rows)
                reads.append(
                    pltpu.make_async_copy(
                        blocks[which].at[half, at], held.at[which, half, at], sems.at[len(reads)]
                    )
                )
    for read in reads:
        read.start()
    for which in range(count):
        total = None
        for half in range(N_X):
            slot = (which * N_X + half) * SPLIT
            for read in reads[slot : slot + SPLIT]:
                read.wait()
            term = jnp.dot(held[which, half], weight_ref[half], preferred_element_type=jnp.float32)
            total = term if total is None else total + term
        parts[which][...] = total.astype(jnp.bfloat16)


def key_parts(blocks, weight, *after):
    count = len(blocks)
    rows = blocks[0].shape[1]
    return pl.pallas_call(
        functools.partial(part_kernel, count),
        in_specs=[HBM] * count + [VMEM] + [ANY] * len(after),
        out_specs=[VMEM] * count,
        out_shape=[jax.ShapeDtypeStruct((rows, weight.shape[2]), jnp.bfloat16)] * count,
        scratch_shapes=[
            pltpu.VMEM((count,) + blocks[0].shape, jnp.bfloat16),
            pltpu.SemaphoreType.DMA((count * N_X * SPLIT,)),
        ],
        compiler_params=PARAMS,
        cost_estimate=COST,
        name="part",
    )(*(in_hbm(one) for one in blocks), weight, *after)


HALVES = 2


def cot_kernel(*refs):
    sources, halves, held, sems = refs[:5], refs[-6 - HALVES : -6], refs[-6:-1], refs[-1]
    reads = [pltpu.make_async_copy(source, target, sems.at[i]) for i, (source, target) in enumerate(zip(sources, held))]
    for read in reads:
        read.start()
    for read in reads:
        read.wait()
    base, factor, first, second, third = held
    width = halves[0].shape[0]
    wide = jnp.concatenate([factor[...]] * (width // BLOCK), axis=1)
    for half, out_ref in enumerate(halves):
        at = pl.ds(half * width, width)
        others = (
            first[:, at].astype(jnp.float32)
            + second[:, at].astype(jnp.float32)
            + third[:, at].astype(jnp.float32)
        )
        out_ref[...] = (base[:, at] + wide * others).T.astype(jnp.bfloat16)


def cotangent(base, factor, parts, *after):
    rows, width = base.shape
    sources = [base, factor, *parts]
    return pl.pallas_call(
        cot_kernel,
        in_specs=[HBM] * 5 + [ANY] * len(after),
        out_specs=[VMEM] * HALVES,
        out_shape=[jax.ShapeDtypeStruct((width // HALVES, rows), jnp.bfloat16)] * HALVES,
        scratch_shapes=[pltpu.VMEM(one.shape, one.dtype) for one in sources] + [pltpu.SemaphoreType.DMA((5,))],
        compiler_params=PARAMS,
        cost_estimate=COST,
        name="cot",
    )(*(in_hbm(one) for one in sources), *after)


def add_kernel(half, own_ref, theirs_ref, *refs):
    out_ref, held, total, in_sems, out_sems = refs[-5:]
    rows, width = theirs_ref.shape
    piece = rows // PIECES
    columns = pl.ds(half * width, width)
    reads, writes = [], []
    for which in range(PIECES):
        at = pl.ds(which * piece, piece)
        reads.append(pltpu.make_async_copy(theirs_ref.at[at], held.at[at], in_sems.at[which]))
        writes.append(pltpu.make_async_copy(total.at[at], out_ref.at[at, columns], out_sems.at[which]))
    for read in reads:
        read.start()
    for which in range(PIECES):
        at = pl.ds(which * piece, piece)
        reads[which].wait()
        total[at, :] = (own_ref[at, columns] + held[at, :].astype(jnp.float32)).astype(jnp.bfloat16)
        writes[which].start()
    for write in writes:
        write.wait()


def add_half(half, own, theirs, before, *after):
    rows, width = theirs.shape
    return pl.pallas_call(
        functools.partial(add_kernel, half),
        in_specs=[VMEM, ANY] + [HBM] * (before is not None) + [ANY] * len(after),
        out_specs=HBM,
        out_shape=jax.ShapeDtypeStruct(own.shape, jnp.bfloat16),
        input_output_aliases={} if before is None else {2: 0},
        scratch_shapes=[
            pltpu.VMEM(theirs.shape, jnp.bfloat16),
            pltpu.VMEM(theirs.shape, jnp.bfloat16),
            pltpu.SemaphoreType.DMA((PIECES,)),
            pltpu.SemaphoreType.DMA((PIECES,)),
        ],
        compiler_params=PARAMS,
        name="add",
    )(own, theirs, *(() if before is None else (before,)), *(in_hbm(one) for one in after))


TILES = 2


def load_kernel(count, half_ref, *refs):
    sources, gain_ref, (held, gain, sems) = refs[:count], refs[count], refs[-3:]
    half = half_ref[0]
    tokens = sources[0].shape[1]
    reads = [pltpu.make_async_copy(gain_ref.at[half], gain, sems.at[count])]
    for which in range(count):
        at = pl.ds(which * tokens, tokens)
        reads.append(pltpu.make_async_copy(sources[which].at[half], held.at[at], sems.at[which]))
    for read in reads:
        read.start()
    for read in reads:
        read.wait()


def load_half(blocks, gain, half, *after):
    count = len(blocks)
    _, tokens, rows = blocks[0].shape
    return pl.pallas_call(
        functools.partial(load_kernel, count),
        in_specs=[SMEM] + [HBM] * (count + 1) + [ANY] * len(after),
        out_specs=[VMEM] * 2,
        out_shape=[pltpu.VMEM((count * tokens, rows), jnp.bfloat16), pltpu.VMEM(gain.shape[1:], gain.dtype)],
        scratch_shapes=[pltpu.SemaphoreType.DMA((count + 1,))],
        compiler_params=PARAMS,
        name="load",
    )(half.reshape(1), *(in_hbm(one) for one in (*blocks, gain)), *after)


def grad_tiles(block_ref, gain_ref, cots, out_ref, group):
    width = cots[0].shape[0]
    tile = out_ref.shape[0] // TILES
    cot = jnp.concatenate([ref[...] for ref in cots], axis=1)
    for part in range(TILES):
        at = pl.ds(part * tile, tile)
        factor = jnp.concatenate([gain_ref[at, :]] * (width // BLOCK), axis=1)
        total = jnp.dot(cot, block_ref[:, at], preferred_element_type=jnp.float32).T * factor
        out_ref[at, pl.ds(group * width, width)] = total.astype(out_ref.dtype)


def grad_kernel(block_ref, gain_ref, *refs):
    grad_tiles(block_ref, gain_ref, refs[:-1], refs[-1], 0)


def sent_grad(block, gain, cots):
    return pl.pallas_call(
        grad_kernel,
        in_specs=[VMEM] * (2 + len(cots)),
        out_specs=VMEM,
        out_shape=jax.ShapeDtypeStruct((block.shape[1], cots[0].shape[0]), jnp.bfloat16),
        compiler_params=PARAMS,
        name="grad",
    )(block, gain, *cots)


def kept_kernel(count, half_ref, *refs):
    sources, gain_ref, refs = refs[:count], refs[count], refs[count + 1 :]
    cots, (out_ref, held, gain, sems) = refs[: HALVES * count], refs[-4:]
    load_kernel(count, half_ref, *sources, gain_ref, held, gain, sems)
    for group in range(HALVES):
        grad_tiles(held, gain, cots[group * count : (group + 1) * count], out_ref, group)


def kept_grad(blocks, gain, half, cots, *after):
    count = len(blocks)
    _, tokens, rows = blocks[0].shape
    width = cots[0][0].shape[0]
    return pl.pallas_call(
        functools.partial(kept_kernel, count),
        in_specs=[SMEM] + [HBM] * (count + 1) + [VMEM] * (HALVES * count) + [ANY] * len(after),
        out_specs=VMEM,
        out_shape=pltpu.VMEM((rows, HALVES * width), jnp.float32),
        scratch_shapes=[
            pltpu.VMEM((count * tokens, rows), jnp.bfloat16),
            pltpu.VMEM(gain.shape[1:], gain.dtype),
            pltpu.SemaphoreType.DMA((count + 1,)),
        ],
        compiler_params=PARAMS,
        cost_estimate=SHORT,
        name="kept",
    )(half.reshape(1), *(in_hbm(one) for one in (*blocks, gain)), *(one for part in cots for one in part), *after)


def per_device(
    activations, norm_gain, key_weight, key_target, replica_frag, outer_params, outer_moment
):
    place = lax.axis_index("fsdp")
    y = place // N_X
    x = place % N_X
    tokens = activations[0]
    quarter = tokens.shape[1] // N_Y
    rows = quarter // N_X
    token_count = tokens.shape[0] * lax.axis_size("fsdp")

    places = {step: lax.rem(y + step, N_Y) for step in (2, 1, 3)}
    sent = {}
    (sent[2],) = cut_columns(tokens, [places[2]], quarter, 0)
    held = {2: send_y(sent[2], 2)}

    fragment, weight = behind([replica_frag[0], key_weight[0]], sent[2])
    frags = lax.all_to_all(fragment, "rep", 0, 0, tiled=True)
    frags = frags.reshape(lax.axis_size("rep"), -1, fragment.shape[1])

    sent[1], sent[3], own = cut_columns(
        tokens, [places[1], places[3], y], quarter, 0, fragment
    )
    held[1], held[3] = send_y(sent[1], 1), send_y(sent[3], 3)
    other = lax.ppermute(weight, "fsdp", X_SWAP)

    gain = lax.dynamic_slice(norm_gain, (y * quarter,), (quarter,))
    wide_gain = jnp.broadcast_to(gain.reshape(N_X, rows, 1), (N_X, rows, BLOCK))
    pair = scaled_pair(x, weight, other, wide_gain)
    base, factor = own_part(tokens, own, pair, key_target[0], token_count)
    parts = {}
    (parts[2],) = key_parts([held[2]], pair, base)
    new_params, new_moment, fresh = outer_step(frags, outer_params, outer_moment, parts[2])
    parts[1], parts[3] = key_parts([held[1], held[3]], pair, fresh)
    chips = lax.axis_size("rep") // N_CORE
    many = spread(fresh, chips, parts[3])
    others = [send_y(parts[step], N_Y - step) for step in (2, 1, 3)]
    cot = cotangent(base, factor, others, many)
    cots = [[part] + [send_y(part, step) for step in (2, 1, 3)] for part in cot]

    cores = [[chip * N_CORE + core for chip in range(chips)] for core in range(N_CORE)]
    own_rows, cols = fresh.shape
    mine = lax.all_to_all(
        many.reshape(chips * own_rows, cols),
        "rep",
        0,
        0,
        axis_index_groups=cores,
        tiled=True,
    ).reshape(chips, own_rows, cols)
    theirs = lax.ppermute(mine, "rep", [(i, i ^ 1) for i in range(chips * N_CORE)])
    fresh_frag = merge_cores(lax.axis_index("rep") % N_CORE, mine, theirs).reshape(-1, cols)

    blocks = [own, held[2], held[1], held[3]]
    theirs, last = [], None
    loaded = load_half(blocks, wide_gain, 1 - x, cot[0])
    for half in range(HALVES):
        last = sent_grad(*loaded, cots[half])
        theirs.append(lax.ppermute(last, "fsdp", X_SWAP))
    mine_grad = kept_grad(blocks, wide_gain, x, cots, last)
    weight_grad = add_half(0, mine_grad, theirs[0], None)
    weight_grad = add_half(1, mine_grad, theirs[1], weight_grad, fresh_frag)
    return (new_params, new_moment, fresh_frag, weight_grad[None])


def solution(mesh):
    placed = (
        P("rep", "fsdp", None),
        P(),
        P("rep", "fsdp", None),
        P("rep", "fsdp", None),
        P("rep", "fsdp", None),
        P(("fsdp", "rep"), None),
        P(("fsdp", "rep"), None),
    )
    return jax.shard_map(
        per_device,
        mesh=mesh,
        in_specs=placed,
        out_specs=(
            P(("fsdp", "rep"), None),
            P(("fsdp", "rep"), None),
            P("fsdp", None),
            P("rep", "fsdp", None),
        ),
        check_vma=False,
    )
```

```python
import functools

import jax
import jax.numpy as jnp
from jax import lax
from jax.experimental import pallas as pl
from jax.experimental.pallas import tpu as pltpu
from jax.sharding import PartitionSpec as P

BLOCK = 128
N_Y = 4
N_X = 2
PER_STEP = 16
N_CORE = 2
ANY = pl.BlockSpec(memory_space=pl.ANY)
HBM = pl.BlockSpec(memory_space=pltpu.HBM)
VMEM = pl.BlockSpec(memory_space=pltpu.VMEM)
SMEM = pl.BlockSpec(memory_space=pltpu.SMEM)
PARAMS = pltpu.CompilerParams(vmem_limit_bytes=24 * 2**20)
COST = pl.CostEstimate(flops=10**12, bytes_accessed=10**9, transcendentals=10**9)
SHORT = pl.CostEstimate(flops=2 * 10**10, bytes_accessed=10**6, transcendentals=0)


def in_hbm(array):
    return pltpu.with_memory_space_constraint(array, pltpu.HBM)


def y_shift(step):
    return [
        (y * N_X + x, ((y + step) % N_Y) * N_X + x) for y in range(N_Y) for x in range(N_X)
    ]


X_SWAP = [(y * N_X + x, y * N_X + 1 - x) for y in range(N_Y) for x in range(N_X)]


def send_y(block, step):
    return lax.ppermute(block, "fsdp", y_shift(step))


def power_not_below(needed):
    scale = jnp.full(needed.shape, 2.0**-30, jnp.float32)
    inverse = jnp.full(needed.shape, 2.0**30, jnp.float32)
    rest = needed
    for step in (32, 16, 8, 4, 2, 1):
        above = rest > 2.0 ** (step - 31)
        scale = jnp.where(above, scale * 2.0**step, scale)
        inverse = jnp.where(above, inverse * 2.0**-step, inverse)
        rest = jnp.where(above, rest * 2.0**-step, rest)
    return scale, inverse


def grid_steps(scaled):
    zeros = lax.clz(jnp.maximum(scaled.astype(jnp.int32), 2))
    spacing = lax.shift_right_logical(jnp.full_like(zeros, 2**30), zeros).astype(jnp.float32)
    inverse = lax.shift_left(jnp.ones_like(zeros), zeros).astype(jnp.float32) * 2.0**-28
    return spacing, scaled * inverse


def outer_kernel(
    replicas, frag_ref, params_ref, moment_ref, *refs
):
    new_params_ref, new_moment_ref, fresh_ref, total = refs[-4:]
    step = pl.program_id(0)

    @pl.when(step == 0)
    def start():
        total[...] = jnp.zeros_like(total)

    rows, cols = params_ref.shape
    blocks = cols // BLOCK
    lane = lax.broadcasted_iota(jnp.int32, (rows, BLOCK), 1)

    def delta(replica, block):
        at = pl.ds(block * BLOCK, BLOCK)
        return params_ref[:, at] - frag_ref[replica, :, at].astype(jnp.float32)

    largest = jnp.zeros((rows, BLOCK), jnp.float32)
    for replica in range(PER_STEP):
        for block in range(blocks):
            peak = jnp.max(jnp.abs(delta(replica, block)), axis=1, keepdims=True)
            largest = jnp.where(lane == replica * blocks + block, peak, largest)
    scales, inverses = power_not_below((largest + 1e-06) / 448.0)
    scales, inverses = scales * 2.0**-9, inverses * 128.0
    for block in range(blocks):
        at = pl.ds(block * BLOCK, BLOCK)
        term = total[:, at]
        for replica in range(PER_STEP):
            slot = replica * blocks + block
            diff = delta(replica, block)
            spacing, steps = grid_steps(jnp.abs(diff) * inverses[:, slot : slot + 1])
            decoded = jnp.floor(steps + 0.5) * (spacing * scales[:, slot : slot + 1])
            term = term + jnp.where(diff < 0, -decoded, decoded)
        total[:, at] = term

    @pl.when(step == pl.num_programs(0) - 1)
    def finish():
        mean_delta = total[...] / jnp.float32(replicas)
        new_moment = 0.9 * moment_ref[...] + mean_delta
        new_params = params_ref[...] - 0.7 * (mean_delta + 0.9 * new_moment)
        new_moment_ref[...] = new_moment
        new_params_ref[...] = new_params
        fresh_ref[...] = new_params.astype(jnp.bfloat16)


def outer_step(frags, outer_params, outer_moment, *after):
    replicas, rows, cols = frags.shape
    whole = pl.BlockSpec((rows, cols), lambda i: (0, 0))
    return pl.pallas_call(
        functools.partial(outer_kernel, replicas),
        grid=(replicas // PER_STEP,),
        in_specs=[pl.BlockSpec((PER_STEP, rows, cols), lambda i: (i, 0, 0)), whole, whole] + [ANY] * len(after),
        out_specs=[whole, whole, whole],
        out_shape=[
            jax.ShapeDtypeStruct((rows, cols), jnp.float32),
            jax.ShapeDtypeStruct((rows, cols), jnp.float32),
            jax.ShapeDtypeStruct((rows, cols), jnp.bfloat16),
        ],
        scratch_shapes=[pltpu.VMEM((rows, cols), jnp.float32)],
        compiler_params=PARAMS,
        cost_estimate=COST,
        name="outer",
    )(frags, outer_params, outer_moment, *after)


def spread_kernel(source_ref, *refs):
    target_ref = refs[-1]
    for copy in range(target_ref.shape[0]):
        target_ref[copy] = source_ref[...]


def spread(source, copies, *after):
    shape = (copies,) + source.shape
    return pl.pallas_call(
        spread_kernel,
        in_specs=[VMEM] + [ANY] * len(after),
        out_specs=VMEM,
        out_shape=pltpu.VMEM(shape, source.dtype),
        compiler_params=PARAMS,
        cost_estimate=COST,
        name="spread",
    )(source, *after)


PIECES = 4


def merge_kernel(core_ref, mine_ref, theirs_ref, out_ref, held, in_sems, out_sems):
    core = core_ref[0]
    chips = held.shape[1] // PIECES
    reads, writes = [], []
    for piece in range(PIECES):
        at = pl.ds(piece * chips, chips)
        for which, (source, slot) in enumerate(((mine_ref, core), (theirs_ref, 1 - core))):
            sem = which * PIECES + piece
            reads.append(pltpu.make_async_copy(source.at[at], held.at[which, at], in_sems.at[sem]))
            writes.append(
                pltpu.make_async_copy(held.at[which, at], out_ref.at[at, slot], out_sems.at[sem])
            )
    for read in reads:
        read.start()
    for read, write in zip(reads, writes):
        read.wait()
        write.start()
    for write in writes:
        write.wait()


def merge_cores(core, mine, theirs):
    chips, rows, cols = mine.shape
    return pl.pallas_call(
        merge_kernel,
        in_specs=[SMEM, ANY, ANY],
        out_specs=HBM,
        out_shape=jax.ShapeDtypeStruct((chips, N_CORE, rows, cols), mine.dtype),
        scratch_shapes=[
            pltpu.VMEM((N_CORE,) + mine.shape, mine.dtype),
            pltpu.SemaphoreType.DMA((N_CORE * PIECES,)),
            pltpu.SemaphoreType.DMA((N_CORE * PIECES,)),
        ],
        compiler_params=PARAMS,
        name="merge",
    )(core.reshape(1), mine, theirs)


def cut_kernel(count, kept, at_ref, source_ref, *refs):
    targets, (buffer, in_sems, out_sems) = refs[-3 - count : -3], refs[-3:]
    width = buffer.shape[3]
    reads, writes = [], []
    for which in range(count):
        for half in range(N_X):
            columns = pl.ds(pl.multiple_of((at_ref[which] * N_X + half) * width, width), width)
            slot = which * N_X + half
            held = buffer.at[which, half] if which < count - kept else targets[which].at[half]
            reads.append(pltpu.make_async_copy(source_ref.at[:, columns], held, in_sems.at[slot]))
            if which < count - kept:
                writes.append(pltpu.make_async_copy(held, targets[which].at[half], out_sems.at[slot]))
    for read in reads:
        read.start()
    for slot, read in enumerate(reads):
        read.wait()
        if slot < len(writes):
            writes[slot].start()
    for write in writes:
        write.wait()


def cut_columns(tokens, places, width, kept, *after):
    rows = tokens.shape[0]
    count = len(places)
    moved = count - kept
    shape = (N_X, rows, width // N_X)
    return pl.pallas_call(
        functools.partial(cut_kernel, count, kept),
        in_specs=[SMEM, HBM] + [ANY] * len(after),
        out_specs=[HBM] * moved + [VMEM] * kept,
        out_shape=[jax.ShapeDtypeStruct(shape, tokens.dtype)] * moved + [pltpu.VMEM(shape, tokens.dtype)] * kept,
        scratch_shapes=[
            pltpu.VMEM((moved,) + shape, tokens.dtype),
            pltpu.SemaphoreType.DMA((count * N_X,)),
            pltpu.SemaphoreType.DMA((moved * N_X,)),
        ],
        compiler_params=PARAMS,
        cost_estimate=COST,
        name="cut",
    )(jnp.stack(places), in_hbm(tokens), *(in_hbm(one) for one in after))


def behind_kernel(count, *refs):
    sources, refs = refs[:count], refs[-2 * count - 2 :]
    targets, buffers, (in_sems, out_sems) = refs[:count], refs[count : 2 * count], refs[2 * count :]
    reads, writes = [], []
    for which in range(count):
        rows = sources[which].shape[0] // PIECES
        for piece in range(PIECES):
            at = pl.ds(piece * rows, rows)
            held = buffers[which].at[at]
            slot = which * PIECES + piece
            reads.append(pltpu.make_async_copy(sources[which].at[at], held, in_sems.at[slot]))
            writes.append(pltpu.make_async_copy(held, targets[which].at[at], out_sems.at[slot]))
    for read in reads:
        read.start()
    for read, write in zip(reads, writes):
        read.wait()
        write.start()
    for write in writes:
        write.wait()


def behind(sources, *after):
    count = len(sources)
    return pl.pallas_call(
        functools.partial(behind_kernel, count),
        in_specs=[HBM] * count + [ANY] * len(after),
        out_specs=[HBM] * count,
        out_shape=[jax.ShapeDtypeStruct(one.shape, one.dtype) for one in sources],
        scratch_shapes=[pltpu.VMEM(one.shape, one.dtype) for one in sources]
        + [pltpu.SemaphoreType.DMA((count * PIECES,))] * 2,
        compiler_params=PARAMS,
        cost_estimate=COST,
        name="behind",
    )(*(in_hbm(one) for one in sources), *(in_hbm(one) for one in after))


def pair_kernel(x_ref, weight_ref, other_ref, gain_ref, pair_ref):
    x = x_ref[0]
    width = weight_ref.shape[1]
    for which, source in enumerate((weight_ref, other_ref)):
        at = x if which == 0 else 1 - x
        factor = jnp.concatenate([gain_ref[at]] * (width // BLOCK), axis=1)
        pair_ref[at] = (source[...].astype(jnp.float32) * factor).astype(jnp.bfloat16)


def scaled_pair(x, weight, other, gain):
    return pl.pallas_call(
        pair_kernel,
        in_specs=[SMEM] + [VMEM] * 3,
        out_specs=VMEM,
        out_shape=pltpu.VMEM((N_X,) + weight.shape, weight.dtype),
        compiler_params=PARAMS,
        cost_estimate=COST,
        name="pair",
    )(x.reshape(1), weight, other, gain)


def own_kernel(token_count, tokens_ref, block_ref, weight_ref, key_target_ref, base_ref, factor_ref):
    wide = tokens_ref[...].astype(jnp.float32)
    inv_rms = lax.rsqrt(jnp.mean(wide * wide, axis=1, keepdims=True) + 1e-05)
    rows = tokens_ref.shape[0]
    at = pl.ds(pl.multiple_of(pl.program_id(0) * rows, rows), rows)
    keys = sum(
        jnp.dot(block_ref[half, at, :], weight_ref[half], preferred_element_type=jnp.float32)
        for half in range(N_X)
    )
    root = jnp.sqrt(jnp.float32(token_count))
    base_ref[...] = (keys * inv_rms - key_target_ref[...].astype(jnp.float32)) / root * inv_rms
    factor_ref[...] = jnp.broadcast_to(inv_rms * inv_rms / root, factor_ref.shape)


def own_part(tokens, block, weight, key_target, token_count):
    rows, depth = tokens.shape
    width = weight.shape[2]
    part = rows // 3
    return pl.pallas_call(
        functools.partial(own_kernel, token_count),
        grid=(3,),
        in_specs=[
            pl.BlockSpec((part, depth), lambda i: (i, 0)),
            VMEM,
            VMEM,
            pl.BlockSpec((part, width), lambda i: (i, 0)),
        ],
        out_specs=[pl.BlockSpec((part, wide), lambda i: (i, 0)) for wide in (width, BLOCK)],
        out_shape=[jax.ShapeDtypeStruct((rows, wide), jnp.float32) for wide in (width, BLOCK)],
        compiler_params=PARAMS,
        cost_estimate=COST,
        name="own",
    )(in_hbm(tokens), block, weight, in_hbm(key_target))


SPLIT = 4


def part_kernel(count, *refs):
    blocks, weight_ref = refs[:count], refs[count]
    parts, (held, result, sems, out_sems) = refs[-4 - count : -4], refs[-4:]
    rows = held.shape[2] // SPLIT
    reads = []
    for which in range(count):
        for half in range(N_X):
            for piece in range(SPLIT):
                at = pl.ds(piece * rows, rows)
                reads.append(
                    pltpu.make_async_copy(
                        blocks[which].at[half, at], held.at[which, half, at], sems.at[len(reads)]
                    )
                )
    for read in reads:
        read.start()
    for which in range(count):
        total = None
        for half in range(N_X):
            slot = (which * N_X + half) * SPLIT
            for read in reads[slot : slot + SPLIT]:
                read.wait()
            term = jnp.dot(held[which, half], weight_ref[half], preferred_element_type=jnp.float32)
            total = term if total is None else total + term
        result[which] = total.astype(jnp.bfloat16)
        pltpu.make_async_copy(result.at[which], parts[which], out_sems.at[which]).start()
    for which in range(count):
        pltpu.make_async_copy(result.at[which], parts[which], out_sems.at[which]).wait()


def key_parts(blocks, weight, *after):
    count = len(blocks)
    rows = blocks[0].shape[1]
    return pl.pallas_call(
        functools.partial(part_kernel, count),
        in_specs=[HBM] * count + [VMEM] + [ANY] * len(after),
        out_specs=[HBM] * count,
        out_shape=[jax.ShapeDtypeStruct((rows, weight.shape[2]), jnp.bfloat16)] * count,
        scratch_shapes=[
            pltpu.VMEM((count,) + blocks[0].shape, jnp.bfloat16),
            pltpu.VMEM((count, rows, weight.shape[2]), jnp.bfloat16),
            pltpu.SemaphoreType.DMA((count * N_X * SPLIT,)),
            pltpu.SemaphoreType.DMA((count,)),
        ],
        compiler_params=PARAMS,
        cost_estimate=COST,
        name="part",
    )(*(in_hbm(one) for one in blocks), weight, *after)


HALVES = 2


def cot_kernel(*refs):
    sources, halves, held, sems = refs[:5], refs[-6 - HALVES : -6], refs[-6:-1], refs[-1]
    reads = [pltpu.make_async_copy(source, target, sems.at[i]) for i, (source, target) in enumerate(zip(sources, held))]
    for read in reads:
        read.start()
    for read in reads:
        read.wait()
    base, factor, first, second, third = held
    width = halves[0].shape[0]
    wide = jnp.concatenate([factor[...]] * (width // BLOCK), axis=1)
    for half, out_ref in enumerate(halves):
        at = pl.ds(half * width, width)
        others = (
            first[:, at].astype(jnp.float32)
            + second[:, at].astype(jnp.float32)
            + third[:, at].astype(jnp.float32)
        )
        out_ref[...] = (base[:, at] + wide * others).T.astype(jnp.bfloat16)


def cotangent(base, factor, parts, *after):
    rows, width = base.shape
    sources = [base, factor, *parts]
    return pl.pallas_call(
        cot_kernel,
        in_specs=[HBM] * 5 + [ANY] * len(after),
        out_specs=[VMEM] * HALVES,
        out_shape=[jax.ShapeDtypeStruct((width // HALVES, rows), jnp.bfloat16)] * HALVES,
        scratch_shapes=[pltpu.VMEM(one.shape, one.dtype) for one in sources] + [pltpu.SemaphoreType.DMA((5,))],
        compiler_params=PARAMS,
        cost_estimate=COST,
        name="cot",
    )(*(in_hbm(one) for one in sources), *after)


def add_kernel(half, own_ref, theirs_ref, *refs):
    out_ref, held, total, in_sems, out_sems = refs[-5:]
    rows, width = theirs_ref.shape
    piece = rows // PIECES
    columns = pl.ds(half * width, width)
    reads, writes = [], []
    for which in range(PIECES):
        at = pl.ds(which * piece, piece)
        reads.append(pltpu.make_async_copy(theirs_ref.at[at], held.at[at], in_sems.at[which]))
        writes.append(pltpu.make_async_copy(total.at[at], out_ref.at[at, columns], out_sems.at[which]))
    for read in reads:
        read.start()
    for which in range(PIECES):
        at = pl.ds(which * piece, piece)
        reads[which].wait()
        total[at, :] = (own_ref[at, columns] + held[at, :].astype(jnp.float32)).astype(jnp.bfloat16)
        writes[which].start()
    for write in writes:
        write.wait()


def add_half(half, own, theirs, before, *after):
    rows, width = theirs.shape
    return pl.pallas_call(
        functools.partial(add_kernel, half),
        in_specs=[VMEM, ANY] + [HBM] * (before is not None) + [ANY] * len(after),
        out_specs=HBM,
        out_shape=jax.ShapeDtypeStruct(own.shape, jnp.bfloat16),
        input_output_aliases={} if before is None else {2: 0},
        scratch_shapes=[
            pltpu.VMEM(theirs.shape, jnp.bfloat16),
            pltpu.VMEM(theirs.shape, jnp.bfloat16),
            pltpu.SemaphoreType.DMA((PIECES,)),
            pltpu.SemaphoreType.DMA((PIECES,)),
        ],
        compiler_params=PARAMS,
        name="add",
    )(own, theirs, *(() if before is None else (before,)), *(in_hbm(one) for one in after))


TILES = 2


def load_kernel(count, half_ref, *refs):
    sources, gain_ref, (held, gain, sems) = refs[:count], refs[count], refs[-3:]
    half = half_ref[0]
    tokens = sources[0].shape[1]
    reads = [pltpu.make_async_copy(gain_ref.at[half], gain, sems.at[count])]
    for which in range(count):
        at = pl.ds(which * tokens, tokens)
        reads.append(pltpu.make_async_copy(sources[which].at[half], held.at[at], sems.at[which]))
    for read in reads:
        read.start()
    for read in reads:
        read.wait()


def load_half(blocks, gain, half, *after):
    count = len(blocks)
    _, tokens, rows = blocks[0].shape
    return pl.pallas_call(
        functools.partial(load_kernel, count),
        in_specs=[SMEM] + [HBM] * (count + 1) + [ANY] * len(after),
        out_specs=[VMEM] * 2,
        out_shape=[pltpu.VMEM((count * tokens, rows), jnp.bfloat16), pltpu.VMEM(gain.shape[1:], gain.dtype)],
        scratch_shapes=[pltpu.SemaphoreType.DMA((count + 1,))],
        compiler_params=PARAMS,
        name="load",
    )(half.reshape(1), *(in_hbm(one) for one in (*blocks, gain)), *after)


def grad_tiles(block_ref, gain_ref, cots, out_ref, group):
    width = cots[0].shape[0]
    tile = out_ref.shape[0] // TILES
    cot = jnp.concatenate([ref[...] for ref in cots], axis=1)
    for part in range(TILES):
        at = pl.ds(part * tile, tile)
        factor = jnp.concatenate([gain_ref[at, :]] * (width // BLOCK), axis=1)
        total = jnp.dot(cot, block_ref[:, at], preferred_element_type=jnp.float32).T * factor
        out_ref[at, pl.ds(group * width, width)] = total.astype(out_ref.dtype)


def grad_kernel(block_ref, gain_ref, *refs):
    grad_tiles(block_ref, gain_ref, refs[:-1], refs[-1], 0)


def sent_grad(block, gain, cots):
    return pl.pallas_call(
        grad_kernel,
        in_specs=[VMEM] * (2 + len(cots)),
        out_specs=VMEM,
        out_shape=jax.ShapeDtypeStruct((block.shape[1], cots[0].shape[0]), jnp.bfloat16),
        compiler_params=PARAMS,
        cost_estimate=pl.CostEstimate(flops=5 * 10**9, bytes_accessed=10**6, transcendentals=0),
        name="grad",
    )(block, gain, *cots)


def kept_kernel(count, half_ref, *refs):
    sources, gain_ref, refs = refs[:count], refs[count], refs[count + 1 :]
    cots, (out_ref, held, gain, sems) = refs[: HALVES * count], refs[-4:]
    load_kernel(count, half_ref, *sources, gain_ref, held, gain, sems)
    for group in range(HALVES):
        grad_tiles(held, gain, cots[group * count : (group + 1) * count], out_ref, group)


def kept_grad(blocks, gain, half, cots, *after):
    count = len(blocks)
    _, tokens, rows = blocks[0].shape
    width = cots[0][0].shape[0]
    return pl.pallas_call(
        functools.partial(kept_kernel, count),
        in_specs=[SMEM] + [HBM] * (count + 1) + [VMEM] * (HALVES * count) + [ANY] * len(after),
        out_specs=VMEM,
        out_shape=pltpu.VMEM((rows, HALVES * width), jnp.float32),
        scratch_shapes=[
            pltpu.VMEM((count * tokens, rows), jnp.bfloat16),
            pltpu.VMEM(gain.shape[1:], gain.dtype),
            pltpu.SemaphoreType.DMA((count + 1,)),
        ],
        compiler_params=PARAMS,
        cost_estimate=SHORT,
        name="kept",
    )(half.reshape(1), *(in_hbm(one) for one in (*blocks, gain)), *(one for part in cots for one in part), *after)


def per_device(
    activations, norm_gain, key_weight, key_target, replica_frag, outer_params, outer_moment
):
    place = lax.axis_index("fsdp")
    y = place // N_X
    x = place % N_X
    tokens = activations[0]
    quarter = tokens.shape[1] // N_Y
    rows = quarter // N_X
    token_count = tokens.shape[0] * lax.axis_size("fsdp")

    places = {step: lax.rem(y + step, N_Y) for step in (2, 1, 3)}
    sent = {}
    (sent[2],) = cut_columns(tokens, [places[2]], quarter, 0)
    held = {2: send_y(sent[2], 2)}

    fragment, weight = behind([replica_frag[0], key_weight[0]], sent[2])
    frags = lax.all_to_all(fragment, "rep", 0, 0, tiled=True)
    frags = frags.reshape(lax.axis_size("rep"), -1, fragment.shape[1])

    sent[1], sent[3], own = cut_columns(
        tokens, [places[1], places[3], y], quarter, 0, fragment
    )
    held[1], held[3] = send_y(sent[1], 1), send_y(sent[3], 3)
    other = lax.ppermute(weight, "fsdp", X_SWAP)

    gain = lax.dynamic_slice(norm_gain, (y * quarter,), (quarter,))
    wide_gain = jnp.broadcast_to(gain.reshape(N_X, rows, 1), (N_X, rows, BLOCK))
    pair = scaled_pair(x, weight, other, wide_gain)
    base, factor = own_part(tokens, own, pair, key_target[0], token_count)
    parts = {}
    (parts[2],) = key_parts([held[2]], pair, base)
    new_params, new_moment, fresh = outer_step(frags, outer_params, outer_moment, parts[2])
    parts[1], parts[3] = key_parts([held[1], held[3]], pair, fresh)
    chips = lax.axis_size("rep") // N_CORE
    many = spread(fresh, chips, parts[3])
    others = [send_y(parts[step], N_Y - step) for step in (2, 1, 3)]
    cot = cotangent(base, factor, others, many)
    cots = [[part] + [send_y(part, step) for step in (1, 3, 2)] for part in cot]

    cores = [[chip * N_CORE + core for chip in range(chips)] for core in range(N_CORE)]
    own_rows, cols = fresh.shape
    mine = lax.all_to_all(
        many.reshape(chips * own_rows, cols),
        "rep",
        0,
        0,
        axis_index_groups=cores,
        tiled=True,
    ).reshape(chips, own_rows, cols)
    theirs = lax.ppermute(mine, "rep", [(i, i ^ 1) for i in range(chips * N_CORE)])
    fresh_frag = merge_cores(lax.axis_index("rep") % N_CORE, mine, theirs).reshape(-1, cols)

    blocks = [own, held[1], held[3], held[2]]
    theirs, last = [], None
    loaded = load_half(blocks, wide_gain, 1 - x, cot[0])
    for half in range(HALVES):
        last = sent_grad(*loaded, cots[half])
        theirs.append(lax.ppermute(last, "fsdp", X_SWAP))
    mine_grad = kept_grad(blocks, wide_gain, x, cots, last)
    weight_grad = add_half(0, mine_grad, theirs[0], None)
    weight_grad = add_half(1, mine_grad, theirs[1], weight_grad, fresh_frag)
    return (new_params, new_moment, fresh_frag, weight_grad[None])


def solution(mesh):
    placed = (
        P("rep", "fsdp", None),
        P(),
        P("rep", "fsdp", None),
        P("rep", "fsdp", None),
        P("rep", "fsdp", None),
        P(("fsdp", "rep"), None),
        P(("fsdp", "rep"), None),
    )
    return jax.shard_map(
        per_device,
        mesh=mesh,
        in_specs=placed,
        out_specs=(
            P(("fsdp", "rep"), None),
            P(("fsdp", "rep"), None),
            P("fsdp", None),
            P("rep", "fsdp", None),
        ),
        check_vma=False,
    )
```

```python
import functools

import jax
import jax.numpy as jnp
from jax import lax
from jax.experimental import pallas as pl
from jax.experimental.pallas import tpu as pltpu
from jax.sharding import PartitionSpec as P

BLOCK = 128
N_Y = 4
N_X = 2
PER_STEP = 16
N_CORE = 2
ANY = pl.BlockSpec(memory_space=pl.ANY)
HBM = pl.BlockSpec(memory_space=pltpu.HBM)
VMEM = pl.BlockSpec(memory_space=pltpu.VMEM)
SMEM = pl.BlockSpec(memory_space=pltpu.SMEM)
PARAMS = pltpu.CompilerParams(vmem_limit_bytes=24 * 2**20)
COST = pl.CostEstimate(flops=10**12, bytes_accessed=10**9, transcendentals=10**9)
SHORT = pl.CostEstimate(flops=2 * 10**10, bytes_accessed=10**6, transcendentals=0)


def in_hbm(array):
    return pltpu.with_memory_space_constraint(array, pltpu.HBM)


def y_shift(step):
    return [
        (y * N_X + x, ((y + step) % N_Y) * N_X + x) for y in range(N_Y) for x in range(N_X)
    ]


X_SWAP = [(y * N_X + x, y * N_X + 1 - x) for y in range(N_Y) for x in range(N_X)]


def send_y(block, step):
    return lax.ppermute(block, "fsdp", y_shift(step))


def power_not_below(needed):
    scale = jnp.full(needed.shape, 2.0**-30, jnp.float32)
    inverse = jnp.full(needed.shape, 2.0**30, jnp.float32)
    rest = needed
    for step in (32, 16, 8, 4, 2, 1):
        above = rest > 2.0 ** (step - 31)
        scale = jnp.where(above, scale * 2.0**step, scale)
        inverse = jnp.where(above, inverse * 2.0**-step, inverse)
        rest = jnp.where(above, rest * 2.0**-step, rest)
    return scale, inverse


def grid_steps(scaled):
    zeros = lax.clz(jnp.maximum(scaled.astype(jnp.int32), 2))
    spacing = lax.shift_right_logical(jnp.full_like(zeros, 2**30), zeros).astype(jnp.float32)
    inverse = lax.shift_left(jnp.ones_like(zeros), zeros).astype(jnp.float32) * 2.0**-28
    return spacing, scaled * inverse


def outer_kernel(
    replicas, frag_ref, params_ref, moment_ref, *refs
):
    new_params_ref, new_moment_ref, fresh_ref, total = refs[-4:]
    step = pl.program_id(0)

    @pl.when(step == 0)
    def start():
        total[...] = jnp.zeros_like(total)

    rows, cols = params_ref.shape
    blocks = cols // BLOCK
    lane = lax.broadcasted_iota(jnp.int32, (rows, BLOCK), 1)

    def delta(replica, block):
        at = pl.ds(block * BLOCK, BLOCK)
        return params_ref[:, at] - frag_ref[replica, :, at].astype(jnp.float32)

    largest = jnp.zeros((rows, BLOCK), jnp.float32)
    for replica in range(PER_STEP):
        for block in range(blocks):
            peak = jnp.max(jnp.abs(delta(replica, block)), axis=1, keepdims=True)
            largest = jnp.where(lane == replica * blocks + block, peak, largest)
    scales, inverses = power_not_below((largest + 1e-06) / 448.0)
    scales, inverses = scales * 2.0**-9, inverses * 128.0
    for block in range(blocks):
        at = pl.ds(block * BLOCK, BLOCK)
        term = total[:, at]
        for replica in range(PER_STEP):
            slot = replica * blocks + block
            diff = delta(replica, block)
            spacing, steps = grid_steps(jnp.abs(diff) * inverses[:, slot : slot + 1])
            decoded = jnp.floor(steps + 0.5) * (spacing * scales[:, slot : slot + 1])
            term = term + jnp.where(diff < 0, -decoded, decoded)
        total[:, at] = term

    @pl.when(step == pl.num_programs(0) - 1)
    def finish():
        mean_delta = total[...] / jnp.float32(replicas)
        new_moment = 0.9 * moment_ref[...] + mean_delta
        new_params = params_ref[...] - 0.7 * (mean_delta + 0.9 * new_moment)
        new_moment_ref[...] = new_moment
        new_params_ref[...] = new_params
        fresh_ref[...] = new_params.astype(jnp.bfloat16)


def outer_step(frags, outer_params, outer_moment, *after):
    replicas, rows, cols = frags.shape
    whole = pl.BlockSpec((rows, cols), lambda i: (0, 0))
    return pl.pallas_call(
        functools.partial(outer_kernel, replicas),
        grid=(replicas // PER_STEP,),
        in_specs=[pl.BlockSpec((PER_STEP, rows, cols), lambda i: (i, 0, 0)), whole, whole] + [ANY] * len(after),
        out_specs=[whole, whole, whole],
        out_shape=[
            jax.ShapeDtypeStruct((rows, cols), jnp.float32),
            jax.ShapeDtypeStruct((rows, cols), jnp.float32),
            jax.ShapeDtypeStruct((rows, cols), jnp.bfloat16),
        ],
        scratch_shapes=[pltpu.VMEM((rows, cols), jnp.float32)],
        compiler_params=PARAMS,
        cost_estimate=COST,
        name="outer",
    )(frags, outer_params, outer_moment, *after)


def spread_kernel(source_ref, *refs):
    target_ref = refs[-1]
    for copy in range(target_ref.shape[0]):
        target_ref[copy] = source_ref[...]


def spread(source, copies, *after):
    shape = (copies,) + source.shape
    return pl.pallas_call(
        spread_kernel,
        in_specs=[VMEM] + [ANY] * len(after),
        out_specs=VMEM,
        out_shape=pltpu.VMEM(shape, source.dtype),
        compiler_params=PARAMS,
        cost_estimate=COST,
        name="spread",
    )(source, *after)


PIECES = 4


def merge_kernel(core_ref, mine_ref, theirs_ref, out_ref, held, in_sems, out_sems):
    core = core_ref[0]
    chips = held.shape[1] // PIECES
    reads, writes = [], []
    for piece in range(PIECES):
        at = pl.ds(piece * chips, chips)
        for which, (source, slot) in enumerate(((mine_ref, core), (theirs_ref, 1 - core))):
            sem = which * PIECES + piece
            reads.append(pltpu.make_async_copy(source.at[at], held.at[which, at], in_sems.at[sem]))
            writes.append(
                pltpu.make_async_copy(held.at[which, at], out_ref.at[at, slot], out_sems.at[sem])
            )
    for read in reads:
        read.start()
    for read, write in zip(reads, writes):
        read.wait()
        write.start()
    for write in writes:
        write.wait()


def merge_cores(core, mine, theirs):
    chips, rows, cols = mine.shape
    return pl.pallas_call(
        merge_kernel,
        in_specs=[SMEM, ANY, ANY],
        out_specs=HBM,
        out_shape=jax.ShapeDtypeStruct((chips, N_CORE, rows, cols), mine.dtype),
        scratch_shapes=[
            pltpu.VMEM((N_CORE,) + mine.shape, mine.dtype),
            pltpu.SemaphoreType.DMA((N_CORE * PIECES,)),
            pltpu.SemaphoreType.DMA((N_CORE * PIECES,)),
        ],
        compiler_params=PARAMS,
        name="merge",
    )(core.reshape(1), mine, theirs)


def cut_kernel(count, kept, at_ref, source_ref, *refs):
    targets, (buffer, in_sems, out_sems) = refs[-3 - count : -3], refs[-3:]
    width = buffer.shape[3]
    reads, writes = [], []
    for which in range(count):
        for half in range(N_X):
            columns = pl.ds(pl.multiple_of((at_ref[which] * N_X + half) * width, width), width)
            slot = which * N_X + half
            held = buffer.at[which, half] if which < count - kept else targets[which].at[half]
            reads.append(pltpu.make_async_copy(source_ref.at[:, columns], held, in_sems.at[slot]))
            if which < count - kept:
                writes.append(pltpu.make_async_copy(held, targets[which].at[half], out_sems.at[slot]))
    for read in reads:
        read.start()
    for slot, read in enumerate(reads):
        read.wait()
        if slot < len(writes):
            writes[slot].start()
    for write in writes:
        write.wait()


def cut_columns(tokens, places, width, kept, *after):
    rows = tokens.shape[0]
    count = len(places)
    moved = count - kept
    shape = (N_X, rows, width // N_X)
    return pl.pallas_call(
        functools.partial(cut_kernel, count, kept),
        in_specs=[SMEM, HBM] + [ANY] * len(after),
        out_specs=[HBM] * moved + [VMEM] * kept,
        out_shape=[jax.ShapeDtypeStruct(shape, tokens.dtype)] * moved + [pltpu.VMEM(shape, tokens.dtype)] * kept,
        scratch_shapes=[
            pltpu.VMEM((moved,) + shape, tokens.dtype),
            pltpu.SemaphoreType.DMA((count * N_X,)),
            pltpu.SemaphoreType.DMA((moved * N_X,)),
        ],
        compiler_params=PARAMS,
        cost_estimate=COST,
        name="cut",
    )(jnp.stack(places), in_hbm(tokens), *(in_hbm(one) for one in after))


def behind_kernel(count, *refs):
    sources, refs = refs[:count], refs[-2 * count - 2 :]
    targets, buffers, (in_sems, out_sems) = refs[:count], refs[count : 2 * count], refs[2 * count :]
    reads, writes = [], []
    for which in range(count):
        rows = sources[which].shape[0] // PIECES
        for piece in range(PIECES):
            at = pl.ds(piece * rows, rows)
            held = buffers[which].at[at]
            slot = which * PIECES + piece
            reads.append(pltpu.make_async_copy(sources[which].at[at], held, in_sems.at[slot]))
            writes.append(pltpu.make_async_copy(held, targets[which].at[at], out_sems.at[slot]))
    for read in reads:
        read.start()
    for read, write in zip(reads, writes):
        read.wait()
        write.start()
    for write in writes:
        write.wait()


def behind(sources, *after):
    count = len(sources)
    return pl.pallas_call(
        functools.partial(behind_kernel, count),
        in_specs=[HBM] * count + [ANY] * len(after),
        out_specs=[HBM] * count,
        out_shape=[jax.ShapeDtypeStruct(one.shape, one.dtype) for one in sources],
        scratch_shapes=[pltpu.VMEM(one.shape, one.dtype) for one in sources]
        + [pltpu.SemaphoreType.DMA((count * PIECES,))] * 2,
        compiler_params=PARAMS,
        cost_estimate=COST,
        name="behind",
    )(*(in_hbm(one) for one in sources), *(in_hbm(one) for one in after))


def pair_kernel(x_ref, weight_ref, other_ref, gain_ref, pair_ref):
    x = x_ref[0]
    width = weight_ref.shape[1]
    for which, source in enumerate((weight_ref, other_ref)):
        at = x if which == 0 else 1 - x
        factor = jnp.concatenate([gain_ref[at]] * (width // BLOCK), axis=1)
        pair_ref[at] = (source[...].astype(jnp.float32) * factor).astype(jnp.bfloat16)


def scaled_pair(x, weight, other, gain):
    return pl.pallas_call(
        pair_kernel,
        in_specs=[SMEM] + [VMEM] * 3,
        out_specs=VMEM,
        out_shape=pltpu.VMEM((N_X,) + weight.shape, weight.dtype),
        compiler_params=PARAMS,
        cost_estimate=COST,
        name="pair",
    )(x.reshape(1), weight, other, gain)


def own_kernel(token_count, tokens_ref, block_ref, weight_ref, key_target_ref, base_ref, factor_ref):
    wide = tokens_ref[...].astype(jnp.float32)
    inv_rms = lax.rsqrt(jnp.mean(wide * wide, axis=1, keepdims=True) + 1e-05)
    rows = tokens_ref.shape[0]
    at = pl.ds(pl.multiple_of(pl.program_id(0) * rows, rows), rows)
    keys = sum(
        jnp.dot(block_ref[half, at, :], weight_ref[half], preferred_element_type=jnp.float32)
        for half in range(N_X)
    )
    root = jnp.sqrt(jnp.float32(token_count))
    base_ref[...] = (keys * inv_rms - key_target_ref[...].astype(jnp.float32)) / root * inv_rms
    factor_ref[...] = jnp.broadcast_to(inv_rms * inv_rms / root, factor_ref.shape)


def own_part(tokens, block, weight, key_target, token_count):
    rows, depth = tokens.shape
    width = weight.shape[2]
    part = rows // 3
    return pl.pallas_call(
        functools.partial(own_kernel, token_count),
        grid=(3,),
        in_specs=[
            pl.BlockSpec((part, depth), lambda i: (i, 0)),
            VMEM,
            VMEM,
            pl.BlockSpec((part, width), lambda i: (i, 0)),
        ],
        out_specs=[pl.BlockSpec((part, wide), lambda i: (i, 0)) for wide in (width, BLOCK)],
        out_shape=[jax.ShapeDtypeStruct((rows, wide), jnp.float32) for wide in (width, BLOCK)],
        compiler_params=PARAMS,
        cost_estimate=COST,
        name="own",
    )(in_hbm(tokens), block, weight, in_hbm(key_target))


SPLIT = 4


def part_kernel(count, *refs):
    blocks, weight_ref = refs[:count], refs[count]
    parts, (held, result, sems, out_sems) = refs[-4 - count : -4], refs[-4:]
    rows = held.shape[2] // SPLIT
    reads = []
    for which in range(count):
        for half in range(N_X):
            for piece in range(SPLIT):
                at = pl.ds(piece * rows, rows)
                reads.append(
                    pltpu.make_async_copy(
                        blocks[which].at[half, at], held.at[which, half, at], sems.at[len(reads)]
                    )
                )
    for read in reads:
        read.start()
    for which in range(count):
        total = None
        for half in range(N_X):
            slot = (which * N_X + half) * SPLIT
            for read in reads[slot : slot + SPLIT]:
                read.wait()
            term = jnp.dot(held[which, half], weight_ref[half], preferred_element_type=jnp.float32)
            total = term if total is None else total + term
        result[which] = total.astype(jnp.bfloat16)
        pltpu.make_async_copy(result.at[which], parts[which], out_sems.at[which]).start()
    for which in range(count):
        pltpu.make_async_copy(result.at[which], parts[which], out_sems.at[which]).wait()


def key_parts(blocks, weight, *after):
    count = len(blocks)
    rows = blocks[0].shape[1]
    return pl.pallas_call(
        functools.partial(part_kernel, count),
        in_specs=[HBM] * count + [VMEM] + [ANY] * len(after),
        out_specs=[HBM] * count,
        out_shape=[jax.ShapeDtypeStruct((rows, weight.shape[2]), jnp.bfloat16)] * count,
        scratch_shapes=[
            pltpu.VMEM((count,) + blocks[0].shape, jnp.bfloat16),
            pltpu.VMEM((count, rows, weight.shape[2]), jnp.bfloat16),
            pltpu.SemaphoreType.DMA((count * N_X * SPLIT,)),
            pltpu.SemaphoreType.DMA((count,)),
        ],
        compiler_params=PARAMS,
        cost_estimate=COST,
        name="part",
    )(*(in_hbm(one) for one in blocks), weight, *after)


HALVES = 2


def cot_kernel(*refs):
    sources, halves, held, sems = refs[:5], refs[-6 - HALVES : -6], refs[-6:-1], refs[-1]
    reads = [pltpu.make_async_copy(source, target, sems.at[i]) for i, (source, target) in enumerate(zip(sources, held))]
    for read in reads:
        read.start()
    for read in reads:
        read.wait()
    base, factor, first, second, third = held
    width = halves[0].shape[0]
    wide = jnp.concatenate([factor[...]] * (width // BLOCK), axis=1)
    for half, out_ref in enumerate(halves):
        at = pl.ds(half * width, width)
        others = (
            first[:, at].astype(jnp.float32)
            + second[:, at].astype(jnp.float32)
            + third[:, at].astype(jnp.float32)
        )
        out_ref[...] = (base[:, at] + wide * others).T.astype(jnp.bfloat16)


def cotangent(base, factor, parts, *after):
    rows, width = base.shape
    sources = [base, factor, *parts]
    return pl.pallas_call(
        cot_kernel,
        in_specs=[HBM] * 5 + [ANY] * len(after),
        out_specs=[VMEM] * HALVES,
        out_shape=[jax.ShapeDtypeStruct((width // HALVES, rows), jnp.bfloat16)] * HALVES,
        scratch_shapes=[pltpu.VMEM(one.shape, one.dtype) for one in sources] + [pltpu.SemaphoreType.DMA((5,))],
        compiler_params=PARAMS,
        cost_estimate=COST,
        name="cot",
    )(*(in_hbm(one) for one in sources), *after)


def add_kernel(half, own_ref, theirs_ref, *refs):
    out_ref, held, total, in_sems, out_sems = refs[-5:]
    rows, width = theirs_ref.shape
    piece = rows // PIECES
    columns = pl.ds(half * width, width)
    reads, writes = [], []
    for which in range(PIECES):
        at = pl.ds(which * piece, piece)
        reads.append(pltpu.make_async_copy(theirs_ref.at[at], held.at[at], in_sems.at[which]))
        writes.append(pltpu.make_async_copy(total.at[at], out_ref.at[at, columns], out_sems.at[which]))
    for read in reads:
        read.start()
    for which in range(PIECES):
        at = pl.ds(which * piece, piece)
        reads[which].wait()
        total[at, :] = (own_ref[at, columns] + held[at, :].astype(jnp.float32)).astype(jnp.bfloat16)
        writes[which].start()
    for write in writes:
        write.wait()


def add_half(half, own, theirs, before, *after):
    rows, width = theirs.shape
    return pl.pallas_call(
        functools.partial(add_kernel, half),
        in_specs=[VMEM, ANY] + [HBM] * (before is not None) + [ANY] * len(after),
        out_specs=HBM,
        out_shape=jax.ShapeDtypeStruct(own.shape, jnp.bfloat16),
        input_output_aliases={} if before is None else {2: 0},
        scratch_shapes=[
            pltpu.VMEM(theirs.shape, jnp.bfloat16),
            pltpu.VMEM(theirs.shape, jnp.bfloat16),
            pltpu.SemaphoreType.DMA((PIECES,)),
            pltpu.SemaphoreType.DMA((PIECES,)),
        ],
        compiler_params=PARAMS,
        name="add",
    )(own, theirs, *(() if before is None else (before,)), *(in_hbm(one) for one in after))


TILES = 2


def load_kernel(count, half_ref, *refs):
    sources, gain_ref, (held, gain, sems) = refs[:count], refs[count], refs[-3:]
    half = half_ref[0]
    tokens = sources[0].shape[1]
    reads = [pltpu.make_async_copy(gain_ref.at[half], gain, sems.at[count])]
    for which in range(count):
        at = pl.ds(which * tokens, tokens)
        reads.append(pltpu.make_async_copy(sources[which].at[half], held.at[at], sems.at[which]))
    for read in reads:
        read.start()
    for read in reads:
        read.wait()


def load_half(blocks, gain, half, *after):
    count = len(blocks)
    _, tokens, rows = blocks[0].shape
    return pl.pallas_call(
        functools.partial(load_kernel, count),
        in_specs=[SMEM] + [HBM] * (count + 1) + [ANY] * len(after),
        out_specs=[VMEM] * 2,
        out_shape=[pltpu.VMEM((count * tokens, rows), jnp.bfloat16), pltpu.VMEM(gain.shape[1:], gain.dtype)],
        scratch_shapes=[pltpu.SemaphoreType.DMA((count + 1,))],
        compiler_params=PARAMS,
        name="load",
    )(half.reshape(1), *(in_hbm(one) for one in (*blocks, gain)), *after)


def grad_tiles(block_ref, gain_ref, cots, out_ref, group):
    width = cots[0].shape[0]
    tile = out_ref.shape[0] // TILES
    cot = jnp.concatenate([ref[...] for ref in cots], axis=1)
    for part in range(TILES):
        at = pl.ds(part * tile, tile)
        factor = jnp.concatenate([gain_ref[at, :]] * (width // BLOCK), axis=1)
        total = jnp.dot(cot, block_ref[:, at], preferred_element_type=jnp.float32).T * factor
        out_ref[at, pl.ds(group * width, width)] = total.astype(out_ref.dtype)


def grad_kernel(order, block_ref, gain_ref, *refs):
    grad_tiles(block_ref, gain_ref, [refs[order.index(which)] for which in range(len(order))], refs[-1], 0)


def sent_grad(block, gain, cots, order):
    return pl.pallas_call(
        functools.partial(grad_kernel, order),
        in_specs=[VMEM] * (2 + len(cots)),
        out_specs=VMEM,
        out_shape=jax.ShapeDtypeStruct((block.shape[1], cots[0].shape[0]), jnp.bfloat16),
        compiler_params=PARAMS,
        cost_estimate=pl.CostEstimate(flops=5 * 10**9, bytes_accessed=10**6, transcendentals=0),
        name="grad",
    )(block, gain, *(cots[which] for which in order))


def kept_kernel(count, half_ref, *refs):
    sources, gain_ref, refs = refs[:count], refs[count], refs[count + 1 :]
    cots, (out_ref, held, gain, sems) = refs[: HALVES * count], refs[-4:]
    load_kernel(count, half_ref, *sources, gain_ref, held, gain, sems)
    for group in range(HALVES):
        grad_tiles(held, gain, cots[group * count : (group + 1) * count], out_ref, group)


def kept_grad(blocks, gain, half, cots, *after):
    count = len(blocks)
    _, tokens, rows = blocks[0].shape
    width = cots[0][0].shape[0]
    return pl.pallas_call(
        functools.partial(kept_kernel, count),
        in_specs=[SMEM] + [HBM] * (count + 1) + [VMEM] * (HALVES * count) + [ANY] * len(after),
        out_specs=VMEM,
        out_shape=pltpu.VMEM((rows, HALVES * width), jnp.float32),
        scratch_shapes=[
            pltpu.VMEM((count * tokens, rows), jnp.bfloat16),
            pltpu.VMEM(gain.shape[1:], gain.dtype),
            pltpu.SemaphoreType.DMA((count + 1,)),
        ],
        compiler_params=PARAMS,
        cost_estimate=SHORT,
        name="kept",
    )(half.reshape(1), *(in_hbm(one) for one in (*blocks, gain)), *(one for part in cots for one in part), *after)


def per_device(
    activations, norm_gain, key_weight, key_target, replica_frag, outer_params, outer_moment
):
    place = lax.axis_index("fsdp")
    y = place // N_X
    x = place % N_X
    tokens = activations[0]
    quarter = tokens.shape[1] // N_Y
    rows = quarter // N_X
    token_count = tokens.shape[0] * lax.axis_size("fsdp")

    places = {step: lax.rem(y + step, N_Y) for step in (2, 1, 3)}
    sent = {}
    (sent[2],) = cut_columns(tokens, [places[2]], quarter, 0)
    held = {2: send_y(sent[2], 2)}

    fragment, weight = behind([replica_frag[0], key_weight[0]], sent[2])
    frags = lax.all_to_all(fragment, "rep", 0, 0, tiled=True)
    frags = frags.reshape(lax.axis_size("rep"), -1, fragment.shape[1])

    sent[1], sent[3], own = cut_columns(
        tokens, [places[1], places[3], y], quarter, 0, fragment
    )
    held[1], held[3] = send_y(sent[1], 1), send_y(sent[3], 3)
    other = lax.ppermute(weight, "fsdp", X_SWAP)

    gain = lax.dynamic_slice(norm_gain, (y * quarter,), (quarter,))
    wide_gain = jnp.broadcast_to(gain.reshape(N_X, rows, 1), (N_X, rows, BLOCK))
    pair = scaled_pair(x, weight, other, wide_gain)
    base, factor = own_part(tokens, own, pair, key_target[0], token_count)
    parts = {}
    (parts[2],) = key_parts([held[2]], pair, base)
    new_params, new_moment, fresh = outer_step(frags, outer_params, outer_moment, parts[2])
    parts[1], parts[3] = key_parts([held[1], held[3]], pair, fresh)
    chips = lax.axis_size("rep") // N_CORE
    many = spread(fresh, chips, parts[3])
    others = [send_y(parts[step], N_Y - step) for step in (2, 1, 3)]
    cot = cotangent(base, factor, others, many)
    cots = [[part] + [send_y(part, step) for step in (1, 3, 2)] for part in cot]

    cores = [[chip * N_CORE + core for chip in range(chips)] for core in range(N_CORE)]
    own_rows, cols = fresh.shape
    mine = lax.all_to_all(
        many.reshape(chips * own_rows, cols),
        "rep",
        0,
        0,
        axis_index_groups=cores,
        tiled=True,
    ).reshape(chips, own_rows, cols)
    theirs = lax.ppermute(mine, "rep", [(i, i ^ 1) for i in range(chips * N_CORE)])
    fresh_frag = merge_cores(lax.axis_index("rep") % N_CORE, mine, theirs).reshape(-1, cols)

    blocks = [own, held[1], held[3], held[2]]
    theirs, last = [], None
    loaded = load_half(blocks, wide_gain, 1 - x, cot[0])
    for half in range(HALVES):
        last = sent_grad(*loaded, cots[half], ((0, 1, 2, 3), (0, 3, 1, 2))[half])
        theirs.append(lax.ppermute(last, "fsdp", X_SWAP))
    mine_grad = kept_grad(blocks, wide_gain, x, cots, last)
    weight_grad = add_half(0, mine_grad, theirs[0], None)
    weight_grad = add_half(1, mine_grad, theirs[1], weight_grad, fresh_frag)
    return (new_params, new_moment, fresh_frag, weight_grad[None])


def solution(mesh):
    placed = (
        P("rep", "fsdp", None),
        P(),
        P("rep", "fsdp", None),
        P("rep", "fsdp", None),
        P("rep", "fsdp", None),
        P(("fsdp", "rep"), None),
        P(("fsdp", "rep"), None),
    )
    return jax.shard_map(
        per_device,
        mesh=mesh,
        in_specs=placed,
        out_specs=(
            P(("fsdp", "rep"), None),
            P(("fsdp", "rep"), None),
            P("fsdp", None),
            P("rep", "fsdp", None),
        ),
        check_vma=False,
    )
```
